128 devices in a mesh: dp: 64 (over z, y_lo, x, core), tensor: 2 (over y_hi).
Axes of the slice: x: 4, y: 4 (y_hi: 2, y_lo: 2; y = y_hi * 2 + y_lo), z: 4, core: 2. Of those that a mesh axis runs over, the one named last changes fastest.
Arguments:
- tokens: bfloat16 [65536, 8192], P('dp', 'tensor'), may hold values from -16 to 16
- cotangent: bfloat16 [65536, 1024], P('dp'), may hold values from -6 to 6
- old_weight: bfloat16 [2, 4096, 1024], P('tensor', 'dp'), may hold values from -0.0625 to 0.0625
- old_first: float32 [2, 4096, 1024], P('tensor', 'dp'), may hold values from -6 to 6
- old_second: float32 [2, 4096, 1024], P('tensor', 'dp'), may hold values from 0.25 to 4
- landing: int32 [64, 64], replicated, may hold values from 0 to 63, as said below
Outputs:
- keys: bfloat16 [65536, 1024], P('dp', 'tensor')
- back: bfloat16 [65536, 8192], P('dp', 'tensor')
- new_weight: bfloat16 [2, 4096, 1024], P('tensor', 'dp')
- new_first: float32 [2, 4096, 1024], P('tensor', 'dp')
- new_second: float32 [2, 4096, 1024], P('tensor', 'dp')
The draws below stay inside these ranges and needn't reach their ends.
Inputs may be any that keep to these rules, and one draw needn't show every extreme that they name: Every column of landing is a permutation of 0..63.
All inputs are finite; a program needn't handle non-finite values.
Results may differ from the reference program's by a relative error of at most 0.0012.
Values may be sent and summed in bfloat16 or wider, within the bound.
No kernel may reach another device: no remote copies, remote signals or barrier semaphores. Data moves between devices by JAX's collectives and lax.ppermute only.
A program may use at most 128 MiB of HBM per device.

```python
import math
import jax
import jax.numpy as jnp
from jax import lax

D = 8192
KVW = 1024
TOKENS = 65536
HALF = 4096
N_DP = 64
N_TENSOR = 2


def draw_landing(key, part):
    key = jax.random.fold_in(key, 11)
    keys = jax.random.split(key, N_DP)
    columns = jax.vmap(lambda single: jax.random.permutation(single, N_DP))(keys)
    return columns.T.astype(jnp.int32)


def with_spikes(array, key, source, target, shards_of, factor):
    owner, partner = [(jnp.arange(array.shape[position]) // (array.shape[position] // shards_of)).reshape([-1 if axis == position else 1 for axis in range(array.ndim)]) for position in (source, target)]
    chosen = jax.random.permutation(key, shards_of)[partner]
    strong = (owner == chosen) | (owner == (partner + shards_of // 2) % shards_of)
    return jnp.where(strong, factor * array, array)


def steps_of(stream_key, shape, cuts, smallest, top_value):
    gain = 1.0
    for position, blocks in cuts:
        draws = jax.random.uniform(jax.random.fold_in(jax.random.fold_in(stream_key, 6), position), (blocks,), jnp.float32, smallest / len(cuts), top_value / len(cuts))
        gain = gain * jnp.repeat(jnp.exp(draws), shape[position] // blocks).reshape((-1,) + (1,) * (len(shape) - 1 - position))
    return gain


def noise(stream_key, shape, scale, limit, shards=(), kind=jnp.bfloat16):
    array = jax.random.normal(stream_key, shape, jnp.float32) * scale
    if len(shards) > 0:
        array = steps_of(stream_key, shape, shards, -0.22, 0.18) * array
    return jnp.clip(array, min=-limit, max=limit).astype(kind)


def gaussian_with(rng, shape, deviation, bound, shards, heavy, kind=jnp.bfloat16):
    entries = deviation * jax.random.normal(rng, shape, jnp.float32)
    if shards:
        entries = entries * steps_of(rng, shape, shards, -0.22, 0.18)
    return jnp.clip(with_spikes(entries, jax.random.fold_in(rng, 3), *heavy), -bound, bound).astype(kind)


def setup_inputs(seed: int = 0) -> dict:
    streams_of = jax.random.split(jax.random.key(seed), 7)
    tokens = gaussian_with(streams_of[0], (TOKENS, D), 1.0, 16.0, ((0, 64), (1, 2)), (0, 1, 64, 4.0))
    cotangent = noise(streams_of[1], (TOKENS, KVW), 1.0, 6.0, ((0, 64),))
    old_weight = noise(streams_of[2], (N_TENSOR, HALF, KVW), D ** -0.5, 0.0625, ((0, 2), (1, 64)))
    old_first = noise(streams_of[3], (N_TENSOR, HALF, KVW), 1.0, 6.0, ((0, 2), (1, 64)), jnp.float32)
    old_second = jnp.clip(jnp.exp(math.log(4.0) - 2.7725887 * jax.random.uniform(streams_of[4], (N_TENSOR, HALF, KVW), jnp.float32) ** steps_of(streams_of[4], (N_TENSOR, HALF, KVW), ((0, 2), (1, 64)), -0.2, 0.2)), 0.25, 4.0)
    landing = draw_landing(jax.random.fold_in(streams_of[6], 71), 0)
    return {"tokens": tokens, "cotangent": cotangent, "old_weight": old_weight, "old_first": old_first, "old_second": old_second, "landing": landing}


beta_first = 0.9
beta_second = 0.95
learn_rate = 0.001
decay_rate = 0.1
epsilon = 1e-08
bias_first = 1.0 - math.exp(100.0 * math.log(beta_first))
bias_second = 1.0 - math.exp(100.0 * math.log(beta_second))

def positions(landing):
    count = landing.shape[0]
    lanes = jnp.arange(count, dtype=jnp.int32)
    hits = landing[None, :, :] == lanes[:, None, None]
    source = lax.optimization_barrier(jnp.sum(jnp.where(hits, lanes[None, :, None], 0), axis=1)).astype(jnp.int32)
    newidx = (lanes[None, :] * count + landing).reshape(-1).astype(jnp.int32)
    oldidx = (source * count + lanes[None, :]).T.reshape(-1).astype(jnp.int32)
    return (source, newidx, oldidx)

def reorder(stack, landing):
    count = landing.shape[0]
    _, _, oldidx = positions(landing)
    halves, rows, width = stack.shape
    blocks = stack.reshape(halves, count * count, rows // (count * count), width)
    return jnp.take(blocks, oldidx, axis=1).reshape(halves, rows, width)

def reference(tokens, cotangent, old_weight, old_first, old_second, landing):
    weight = reorder(old_weight, landing)
    first = reorder(old_first, landing)
    second = reorder(old_second, landing)
    full = weight.reshape(D, KVW)
    keys = jnp.dot(tokens, full, preferred_element_type=jnp.float32).astype(jnp.bfloat16)
    back = lax.dot_general(cotangent, full, (((1,), (1,)), ((), ())), preferred_element_type=jnp.float32).astype(jnp.bfloat16)
    grad = lax.dot_general(tokens, cotangent, (((0,), (0,)), ((), ())), preferred_element_type=jnp.float32)
    grad = (grad * (1.0 / math.sqrt(TOKENS))).reshape(weight.shape)
    new_first = beta_first * first + (1.0 - beta_first) * grad
    new_second = beta_second * second + (1.0 - beta_second) * grad * grad
    step = new_first / bias_first / (jnp.sqrt(new_second / bias_second) + epsilon)
    base = weight.astype(jnp.float32)
    new_weight = (base - learn_rate * (step + decay_rate * base)).astype(jnp.bfloat16)
    return (keys, back, new_weight, new_first, new_second)
```

```python
import math

import jax
import jax.numpy as jnp
from jax import lax
from jax.experimental import pallas as pl
from jax.experimental.pallas import tpu as pltpu
from jax.sharding import Mesh, PartitionSpec as P

beta_first = 0.9
beta_second = 0.95
learn_rate = 0.001
decay_rate = 0.1
epsilon = 1e-08
bias_first = 1.0 - math.exp(100.0 * math.log(beta_first))
bias_second = 1.0 - math.exp(100.0 * math.log(beta_second))

AXES = ("z", "l", "x", "c", "t")
SIZES = (4, 2, 4, 2, 2)
DP = AXES[:4]
NZ, NL, NX, NC, NT = SIZES
COUNT = NZ * NL * NX * NC
MIB = 1 << 20


def shift(value, axis, step):
    size = SIZES[AXES.index(axis)]
    return lax.ppermute(value, axis, [(i, (i + step) % size) for i in range(size)])


def gather_axis(value, axis):
    return [value] + [shift(value, axis, -k) for k in (1, 2, 3)]


def grad_kernel(place, tokens, cotangent, keep, send, held):
    x, c = place[2], place[3]
    term = lax.dot_general(
        tokens[...], cotangent[...], (((0,), (0,)), ((), ())), preferred_element_type=jnp.float32
    )
    held[...] = term.reshape(held.shape)
    for k in range(NX):
        at = lax.rem(x + k, NX)
        keep[0, k] = held[at, c]
        send[0, k] = held[at, 1 - c].astype(send.dtype)


def local_grad(place, tokens, cotangent):
    rows, half = tokens.shape
    width = cotangent.shape[1]
    groups = NZ * NL
    block = half // groups
    own = half // COUNT

    def columns(k, place):
        return (0, lax.rem(place[0] + k // NL, NZ) * NL + lax.rem(place[1] + k % NL, NL))

    out = (groups, NX, own, width)
    out_spec = pl.BlockSpec((1, NX, own, width), lambda k, place: (k, 0, 0, 0))
    return pl.pallas_call(
        grad_kernel,
        grid_spec=pltpu.PrefetchScalarGridSpec(
            num_scalar_prefetch=1,
            grid=(groups,),
            in_specs=[
                pl.BlockSpec((rows, block), columns),
                pl.BlockSpec((rows, width), lambda k, place: (0, 0)),
            ],
            out_specs=[out_spec, out_spec],
            scratch_shapes=[pltpu.VMEM((NX, NC, own, width), jnp.float32)],
        ),
        out_shape=[
            jax.ShapeDtypeStruct(out, jnp.float32),
            jax.ShapeDtypeStruct(out, jnp.bfloat16),
        ],
        compiler_params=pltpu.CompilerParams(vmem_limit_bytes=40 * MIB),
        cost_estimate=pl.CostEstimate(
            flops=2 * rows * half * width, bytes_accessed=rows * half * 2 + half * width * 3, transcendentals=0
        ),
    )(place, tokens, cotangent)


def keys_kernel(place, target, tokens, *refs):
    pieces, (full, keys_send, keys_keep, held) = refs[:-4], refs[-4:]
    o = pl.program_id(0)
    t = place[4]
    per_half = len(pieces) // 2
    block = full.shape[0]
    width = full.shape[1]

    def work(parts):
        rows = jnp.concatenate([p[...].reshape(-1, width) for p in parts], axis=0)
        pick = lax.broadcasted_iota(jnp.int32, (block, rows.shape[0]), 0) == target[0]
        pick = jnp.where(pick, 1.0, 0.0).astype(jnp.bfloat16)
        moved = jnp.dot(pick, rows, preferred_element_type=jnp.float32).astype(jnp.bfloat16)
        full[...] = moved
        for h in range(NT):
            held[h] = moved[:, h * (width // NT) : (h + 1) * (width // NT)]

    pl.when(o < 4)(lambda: work(pieces[:per_half]))
    pl.when(o >= 4)(lambda: work(pieces[per_half:]))

    @pl.when(o == 0)
    def _():
        keys_send[...] = jnp.zeros_like(keys_send)
        keys_keep[...] = jnp.zeros_like(keys_keep)

    keys_send[...] += jnp.dot(tokens[...], held[1 - t], preferred_element_type=jnp.float32)
    keys_keep[...] += jnp.dot(tokens[...], held[t], preferred_element_type=jnp.float32)


def reorder_and_keys(place, target, tokens, pieces_a, pieces_b):
    rows, half = tokens.shape
    width = pieces_a[0].shape[-1]
    block = half // 8
    inner = pieces_a[0].shape[:2]
    spec_a = pl.BlockSpec((*inner, 1, 8, width), lambda o, place: (0, 0, jnp.minimum(o, 3), 0, 0))
    spec_b = pl.BlockSpec((*inner, 1, 8, width), lambda o, place: (0, 0, jnp.maximum(o, 4) - 4, 0, 0))
    keys_spec = pl.BlockSpec((rows, width // NT), lambda o, place: (0, 0))
    keys_type = jax.ShapeDtypeStruct((rows, width // NT), jnp.float32)
    return pl.pallas_call(
        keys_kernel,
        grid_spec=pltpu.PrefetchScalarGridSpec(
            num_scalar_prefetch=1,
            grid=(8,),
            in_specs=[
                pl.BlockSpec((1, 1, block), lambda o, place: (o, 0, 0)),
                pl.BlockSpec((rows, block), lambda o, place: (0, o)),
            ]
            + [spec_a] * len(pieces_a)
            + [spec_b] * len(pieces_b),
            out_specs=[pl.BlockSpec((block, width), lambda o, place: (o, 0)), keys_spec, keys_spec],
            scratch_shapes=[pltpu.VMEM((NT, block, width // NT), jnp.bfloat16)],
        ),
        out_shape=[jax.ShapeDtypeStruct((half, width), jnp.bfloat16), keys_type, keys_type],
        compiler_params=pltpu.CompilerParams(vmem_limit_bytes=48 * MIB),
        cost_estimate=pl.CostEstimate(
            flops=3 * rows * half * width, bytes_accessed=rows * half * 2 + half * width * 6, transcendentals=0
        ),
    )(place, target, tokens, *pieces_a, *pieces_b)


def shards(tokens, cotangent, old_weight, old_first, old_second, landing):
    z, l, x, c, t = [lax.axis_index(a).astype(jnp.int32) for a in AXES]
    place = jnp.stack([z, l, x, c, t])
    me = ((z * NL + l) * NX + x) * NC + c
    rows, width = old_weight.shape[1:]
    scale = 1.0 / math.sqrt(tokens.shape[0] * COUNT)
    half_rows = rows // 2

    own = old_weight.reshape(rows, width)
    other = shift(own, "l", 1)
    pair = jnp.stack([own, other]).reshape(NL, 2, half_rows, width)

    def gathered(part, first, second):
        stage = jnp.stack(gather_axis(part, first))
        here = gather_axis(stage.reshape(NX * NL, half_rows // 8, 8, width), second)
        return here

    part_a = gathered(pair[:, 0], "z", "x")
    part_b = gathered(pair[:, 1], "x", "z")
    pieces_a = [v.reshape(NX, NL, half_rows // 8, 8, width) for v in part_a + [shift(v, "c", 1) for v in part_a]]
    pieces_b = [v.reshape(NX, NL, half_rows // 8, 8, width) for v in part_b + [shift(v, "c", 1) for v in part_b]]

    step4 = jnp.arange(4, dtype=jnp.int32)
    step2 = jnp.arange(2, dtype=jnp.int32)
    xs, zs, ls, cs = (x + step4) % NX, (z + step4) % NZ, (l + step2) % NL, (c + step2) % NC

    def owner(zi, li, xi, ci):
        return ((zi * NL + li) * NX + xi) * NC + ci

    order_a = owner(zs[None, None, :, None], ls[None, None, None, :], xs[None, :, None, None], cs[:, None, None, None])
    order_b = owner(zs[None, :, None, None], ls[None, None, None, :], xs[None, None, :, None], cs[:, None, None, None])

    def targets(order, at):
        spots = jnp.take(landing, order.reshape(-1), axis=0)[:, at : at + half_rows]
        spots = spots.reshape(COUNT, half_rows // 8, 8) + jnp.arange(8, dtype=jnp.int32) * COUNT
        return spots.transpose(1, 0, 2).reshape(half_rows // 8, 1, COUNT * 8)

    target = jnp.concatenate([targets(order_a, 0), targets(order_b, half_rows)])

    moments = jnp.concatenate([old_first.reshape(rows, width), old_second.reshape(rows, width)], axis=1)
    moments = lax.all_to_all(moments, DP, split_axis=0, concat_axis=0, tiled=True)

    keep, send = local_grad(place, tokens, cotangent)
    came = shift(send, "c", 1)
    shape = (NZ, NL, NX, rows, width)
    keep, came = keep.reshape(shape), came.reshape(shape)

    def both(index):
        return keep[index] + came[index].astype(jnp.float32)

    def reduced(terms, axis):
        total = terms[0]
        for k in (1, 2, 3):
            total = total + shift(terms[k].astype(jnp.bfloat16), axis, k).astype(jnp.float32)
        return total

    low, high = slice(0, half_rows), slice(half_rows, rows)
    sum_a = reduced([both((k, slice(None), slice(None), low)) for k in range(4)], "z")
    sum_b = reduced([both((slice(None), slice(None), k, high)) for k in range(4)], "x")
    sum_a = reduced([sum_a[:, k] for k in range(4)], "x")
    sum_b = reduced([sum_b[k] for k in range(4)], "z")
    sums = jnp.concatenate([sum_a, sum_b], axis=1)
    grad = (sums[0] + shift(sums[1].astype(jnp.bfloat16), "l", 1).astype(jnp.float32)) * scale

    full, keys_send, keys_keep = reorder_and_keys(place, target, tokens, pieces_a, pieces_b)
    keys = (keys_keep + shift(keys_send, "t", 1)).astype(jnp.bfloat16)
    back = lax.dot_general(
        cotangent, full, (((1,), (1,)), ((), ())), preferred_element_type=jnp.float32
    ).astype(jnp.bfloat16)

    column = lax.dynamic_slice_in_dim(landing, me, 1, 1)[:, 0]
    lanes = jnp.arange(COUNT, dtype=jnp.int32)
    source = jnp.sum(jnp.where(column[None, :] == lanes[:, None], lanes[None, :], 0), axis=1)
    moments = jnp.take(moments, source, axis=0)
    first_now, second_now = moments[:, :width], moments[:, width:]
    base = lax.dynamic_slice_in_dim(full, me * rows, rows, 0).astype(jnp.float32)
    new_first = beta_first * first_now + (1.0 - beta_first) * grad
    new_second = beta_second * second_now + (1.0 - beta_second) * grad * grad
    step = new_first / bias_first / (jnp.sqrt(new_second / bias_second) + epsilon)
    new_weight = (base - learn_rate * (step + decay_rate * base)).astype(jnp.bfloat16)
    return (keys, back, new_weight[None], new_first[None], new_second[None])


def solution(mesh):
    fine = Mesh(mesh.devices.reshape(SIZES), AXES)
    in_specs = (
        P(DP, "t"),
        P(DP, None),
        P("t", DP, None),
        P("t", DP, None),
        P("t", DP, None),
        P(),
    )
    out_specs = (
        P(DP, "t"),
        P(DP, "t"),
        P("t", DP, None),
        P("t", DP, None),
        P("t", DP, None),
    )
    return jax.shard_map(shards, mesh=fine, in_specs=in_specs, out_specs=out_specs, check_vma=False)
```

```python
import functools
import math

import jax
import jax.numpy as jnp
from jax import lax
from jax.experimental import pallas as pl
from jax.experimental.pallas import tpu as pltpu
from jax.sharding import Mesh, PartitionSpec as P

beta_first = 0.9
beta_second = 0.95
learn_rate = 0.001
decay_rate = 0.1
epsilon = 1e-08
bias_first = 1.0 - math.exp(100.0 * math.log(beta_first))
bias_second = 1.0 - math.exp(100.0 * math.log(beta_second))

AXES = ("z", "l", "x", "c", "t")
SIZES = (4, 2, 4, 2, 2)
DP = AXES[:4]
NZ, NL, NX, NC, NT = SIZES
COUNT = NZ * NL * NX * NC
NG = 2
SLOT = 64
MIB = 1 << 20


def shift(value, axis, step):
    size = SIZES[AXES.index(axis)]
    return lax.ppermute(value, axis, [(i, (i + step) % size) for i in range(size)])


def cross(value, stage, step):
    pairs = []
    for z in range(NZ):
        for x in range(NX):
            for c in range(NC):
                to = ((z + step) % NZ, x) if c == stage else (z, (x + step) % NX)
                pairs.append(((z * NX + x) * NC + c, (to[0] * NX + to[1]) * NC + c))
    return lax.ppermute(value, ("z", "x", "c"), pairs)


def gathered(value, stage):
    return [value] + [cross(value, stage, -k) for k in (1, 2, 3)]


def reduced(terms, stage):
    total = terms[0]
    for k in (1, 2, 3):
        total = total + cross(terms[k], stage, k).astype(jnp.float32)
    return total


def after(value, *others):
    return lax.optimization_barrier((value, *others))[0]


def select_kernel(place, tokens, mine, other):
    z, l, x, c = place[0], place[1], place[2], place[3]
    lanes = NC * SLOT
    below = lax.broadcasted_iota(jnp.int32, (tokens.shape[0], lanes), 1) < SLOT

    def column(core, slot):
        first, pair, second = slot // (NL * 4), slot // 4 % NL, slot % 4
        to_z = lax.rem(z + jnp.where(core == 0, first, second), NZ)
        to_x = lax.rem(x + jnp.where(core == 0, second, first), NX)
        at = (to_z * NL + lax.rem(l + pair, NL)) * NX + to_x
        return tokens[:, pl.ds(pl.multiple_of(at * lanes, lanes), lanes)]

    for core, out in ((c, mine), (1 - c, other)):
        for slot in range(0, COUNT // NC, NC):
            one = pltpu.roll(column(core, slot), SLOT * core, 1)
            two = pltpu.roll(column(core, slot + 1), SLOT * (1 - core), 1)
            out[:, slot * SLOT : (slot + 2) * SLOT] = jnp.where(below, one, two)


def selected(place, tokens):
    rows, half = tokens.shape
    block = 128
    out = jax.ShapeDtypeStruct((rows, half // NC), tokens.dtype)
    spec = pl.BlockSpec((block, half // NC), lambda k, place: (k, 0))
    return pl.pallas_call(
        select_kernel,
        grid_spec=pltpu.PrefetchScalarGridSpec(
            num_scalar_prefetch=1,
            grid=(rows // block,),
            in_specs=[pl.BlockSpec((block, half), lambda k, place: (k, 0))],
            out_specs=[spec, spec],
        ),
        out_shape=[out, out],
        compiler_params=pltpu.CompilerParams(vmem_limit_bytes=10 * MIB),
        cost_estimate=pl.CostEstimate(flops=0, bytes_accessed=4 * rows * half, transcendentals=0),
    )(place, tokens)


def grad_kernel(mine, theirs, cotangent, cotangent_theirs, own, *sends):
    term = lax.dot_general(
        mine[...], cotangent[...], (((0,), (0,)), ((), ())), preferred_element_type=jnp.float32
    )
    term += lax.dot_general(
        theirs[...], cotangent_theirs[...], (((0,), (0,)), ((), ())), preferred_element_type=jnp.float32
    )
    term = term.reshape(own.shape)
    k = pl.program_id(0)

    @pl.when(k == 0)
    def _():
        own[...] = term

    for at, send in enumerate(sends):

        @pl.when(k == at + 1)
        def _():
            send[...] = term.astype(send.dtype)


def chip_grad(mine, theirs, cotangent, cotangent_theirs):
    rows, half = mine.shape
    width = cotangent.shape[1]
    piece = (half // 4 // SLOT, SLOT, width)
    part = pl.BlockSpec((rows, half // 4), lambda k: (0, k))
    whole = pl.BlockSpec((rows, width), lambda k: (0, 0))
    return pl.pallas_call(
        grad_kernel,
        grid=(4,),
        in_specs=[part, part, whole, whole],
        out_specs=[pl.BlockSpec(piece, lambda k: (0, 0, 0))] * 4,
        out_shape=[jax.ShapeDtypeStruct(piece, jnp.bfloat16 if n else jnp.float32) for n in range(4)],
        compiler_params=pltpu.CompilerParams(vmem_limit_bytes=30 * MIB),
        cost_estimate=pl.CostEstimate(
            flops=rows * half * width // 2, bytes_accessed=(rows * half + half * width), transcendentals=0
        ),
    )(mine, theirs, cotangent, cotangent_theirs)


def reorder_kernel(place, target, tokens, *refs):
    pieces, (full, keys_send, held) = refs[:-3], refs[-3:]
    t = place[4]
    block, width = full.shape
    for group in range(NG):
        size = block // NG
        each = pieces[0].shape[0] // NG
        rows = jnp.concatenate(
            [p[group * each : (group + 1) * each].reshape(-1, width) for p in pieces], axis=0
        )
        pick = lax.broadcasted_iota(jnp.int32, (size, rows.shape[0]), 0) == target[group]
        pick = jnp.where(pick, 1.0, 0.0).astype(jnp.bfloat16)
        moved = jnp.dot(pick, rows, preferred_element_type=jnp.float32).astype(jnp.bfloat16)
        at = pl.ds(group * size, size)
        full[at, :] = moved
        for h in range(NT):
            held[h, at, :] = moved[:, h * (width // NT) : (h + 1) * (width // NT)]

    @pl.when(pl.program_id(0) == 0)
    def _():
        keys_send[...] = jnp.zeros_like(keys_send)

    keys_send[...] += jnp.dot(tokens[...], held[1 - t], preferred_element_type=jnp.float32)


def reorder_and_send(place, target, tokens, pieces):
    rows, half = tokens.shape
    width = pieces[0].shape[-1]
    octets = target.shape[0] // NG
    block = half // octets
    lines, line, _ = pieces[0].shape
    piece = pl.BlockSpec((lines // octets, line, width), lambda o, place: (o, 0, 0))
    return pl.pallas_call(
        reorder_kernel,
        grid_spec=pltpu.PrefetchScalarGridSpec(
            num_scalar_prefetch=1,
            grid=(octets,),
            in_specs=[
                pl.BlockSpec((NG, 1, block // NG), lambda o, place: (o, 0, 0)),
                pl.BlockSpec((rows, block), lambda o, place: (0, o)),
            ]
            + [piece] * len(pieces),
            out_specs=[
                pl.BlockSpec((block, width), lambda o, place: (o, 0)),
                pl.BlockSpec((rows, width // NT), lambda o, place: (0, 0)),
            ],
            scratch_shapes=[pltpu.VMEM((NT, block, width // NT), jnp.bfloat16)],
        ),
        out_shape=[
            jax.ShapeDtypeStruct((half, width), jnp.bfloat16),
            jax.ShapeDtypeStruct((rows, width // NT), jnp.float32),
        ],
        compiler_params=pltpu.CompilerParams(vmem_limit_bytes=22 * MIB),
        cost_estimate=pl.CostEstimate(
            flops=2 * rows * half * width, bytes_accessed=rows * half * 2 + half * width * 4, transcendentals=0
        ),
    )(place, target, tokens, *pieces)


def keep_kernel(place, tokens, full, keys):
    @pl.when(pl.program_id(0) == 0)
    def _():
        keys[...] = jnp.zeros_like(keys)

    keys[...] += jnp.dot(tokens[...], full[...], preferred_element_type=jnp.float32)


def keys_kept(place, tokens, full):
    rows, half = tokens.shape
    width = full.shape[1]
    block = 512
    return pl.pallas_call(
        keep_kernel,
        grid_spec=pltpu.PrefetchScalarGridSpec(
            num_scalar_prefetch=1,
            grid=(half // block,),
            in_specs=[
                pl.BlockSpec((rows, block), lambda o, place: (0, o)),
                pl.BlockSpec((block, width // NT), lambda o, place: (o, place[4])),
            ],
            out_specs=pl.BlockSpec((rows, width // NT), lambda o, place: (0, 0)),
        ),
        out_shape=jax.ShapeDtypeStruct((rows, width // NT), jnp.float32),
        compiler_params=pltpu.CompilerParams(vmem_limit_bytes=14 * MIB),
        cost_estimate=pl.CostEstimate(
            flops=0, bytes_accessed=0, transcendentals=0
        ),
    )(place, tokens, full)


def back_kernel(cotangent, full, *refs):
    out = refs[-1]
    out[...] = lax.dot_general(
        cotangent[...], full[...], (((1,), (1,)), ((), ())), preferred_element_type=jnp.float32
    ).astype(out.dtype)


def back_part(cotangent, full, first, last, held):
    rows, width = cotangent.shape
    half = full.shape[0]
    block = 512
    return pl.pallas_call(
        back_kernel,
        grid=(last - first,),
        in_specs=[
            pl.BlockSpec((rows, width), lambda o: (0, 0)),
            pl.BlockSpec((block, width), lambda o: (o + first, 0)),
        ]
        + [pl.BlockSpec(memory_space=pl.ANY)] * len(held),
        out_specs=pl.BlockSpec((rows, block), lambda o: (0, o + first)),
        out_shape=jax.ShapeDtypeStruct((rows, half), jnp.bfloat16),
        input_output_aliases={2: 0} if held else {},
        compiler_params=pltpu.CompilerParams(vmem_limit_bytes=14 * MIB),
        cost_estimate=pl.CostEstimate(
            flops=0, bytes_accessed=0, transcendentals=0
        ),
    )(cotangent, full, *held)


def pack_kernel(first, second, out):
    for n, moment in enumerate((first, second)):
        for k in range(8):
            out[:, n * 8 + k, :] = moment[:, k * 128 : (k + 1) * 128]


def packed(first, second):
    rows, width = first.shape
    return pl.pallas_call(
        pack_kernel,
        out_shape=jax.ShapeDtypeStruct((rows, 16, width // 8), jnp.float32),
        compiler_params=pltpu.CompilerParams(vmem_limit_bytes=4 * MIB),
        cost_estimate=pl.CostEstimate(flops=0, bytes_accessed=4 * MIB // 4, transcendentals=0),
    )(first, second)


def update_kernel(scale, me, source, moments, own, came, full, weight, first, second, held):
    rows = held.shape[0]

    def move(p, carry):
        held[p] = moments[source[p]]
        return carry

    lax.fori_loop(0, rows, move, 0, unroll=8)
    for k in range(8):
        at = slice(k * 128, (k + 1) * 128)
        grad = (own[:, at] + came[:, at].astype(jnp.float32)) * scale
        base = full[:, at].astype(jnp.float32)
        new_first = beta_first * held[:, k, :] + (1.0 - beta_first) * grad
        new_second = beta_second * held[:, 8 + k, :] + (1.0 - beta_second) * grad * grad
        step = new_first / bias_first / (jnp.sqrt(new_second / bias_second) + epsilon)
        weight[:, at] = (base - learn_rate * (step + decay_rate * base)).astype(weight.dtype)
        first[:, at] = new_first
        second[:, at] = new_second


def updated(me, source, moments, own, came, full, scale):
    rows, width = own.shape
    whole = pl.BlockSpec((rows, width), lambda i, me, source: (0, 0))
    return pl.pallas_call(
        functools.partial(update_kernel, scale),
        grid_spec=pltpu.PrefetchScalarGridSpec(
            num_scalar_prefetch=2,
            grid=(1,),
            in_specs=[
                pl.BlockSpec(moments.shape, lambda i, me, source: (0, 0, 0)),
                whole,
                whole,
                pl.BlockSpec((rows, width), lambda i, me, source: (me[0], 0)),
            ],
            out_specs=[whole] * 3,
            scratch_shapes=[pltpu.VMEM(moments.shape, jnp.float32)],
        ),
        out_shape=[jax.ShapeDtypeStruct((rows, width), k) for k in (jnp.bfloat16, jnp.float32, jnp.float32)],
        compiler_params=pltpu.CompilerParams(vmem_limit_bytes=8 * MIB),
        cost_estimate=pl.CostEstimate(flops=0, bytes_accessed=MIB, transcendentals=0),
    )(me, source, moments, own, came, full)


def targets(landing, place, rows):
    z, l, x, c = place[0], place[1], place[2], place[3]
    steps = jnp.arange(4, dtype=jnp.int32)
    zs, xs = (z + steps) % NZ, (x + steps) % NX
    ls = (l + jnp.arange(NL, dtype=jnp.int32)) % NL

    def owners(core):
        along_z = (zs[None, :, None] * NL + ls) * NX + xs[:, None, None]
        along_x = (zs[:, None, None] * NL + ls) * NX + xs[None, :, None]
        return (jnp.where(core == 0, along_z, along_x) * NC + core).reshape(-1)

    order = jnp.concatenate([owners(c), owners(1 - c)])
    groups = 8 * NG
    each = COUNT // groups
    spots = jnp.take(landing, order, axis=0).reshape(COUNT // (4 * NL), 4 * NL, groups, each)
    spots = spots + jnp.arange(each, dtype=jnp.int32) * rows
    return spots.transpose(2, 0, 3, 1).reshape(groups, 1, each * COUNT)


def shards(tokens, cotangent, old_weight, old_first, old_second, landing):
    z, l, x, c, t = [lax.axis_index(a).astype(jnp.int32) for a in AXES]
    place = jnp.stack([z, l, x, c, t])
    me = ((z * NL + l) * NX + x) * NC + c
    rows, width = old_weight.shape[1:]
    scale = 1.0 / math.sqrt(tokens.shape[0] * COUNT)

    own = old_weight.reshape(rows, width)
    pair = jnp.stack([own, shift(own, "l", 1)])
    moments = packed(old_first.reshape(rows, width), old_second.reshape(rows, width))
    target = targets(landing, place, rows)
    pair, moments, target, tokens_1 = lax.optimization_barrier((pair, moments, target, tokens))
    line = jnp.stack(gathered(pair, 0)).reshape(4 * NL, rows, width)
    mine, other = selected(place, tokens_1)
    line, mine, other, cotangent_1, moments = lax.optimization_barrier((line, mine, other, cotangent, moments))
    theirs = shift(other, "c", 1)
    cotangent_theirs = shift(cotangent_1, "c", 1)
    line = line.transpose(1, 0, 2)
    here = gathered(line, 1)
    there = shift(line, "c", 1)
    moments = lax.all_to_all(moments, DP, split_axis=0, concat_axis=0, tiled=True)
    terms = chip_grad(mine, theirs, cotangent, cotangent_theirs)
    here, terms, moments = lax.optimization_barrier((here, terms, moments))
    pieces = here + [there] + [shift(v, "c", 1) for v in here[1:]]

    total = reduced(terms, 0).reshape(NL, 4, rows, width)
    full, keys_send = reorder_and_send(place, target, tokens, pieces)
    keys_came = shift(keys_send, "t", 1)
    keys_keep = keys_kept(place, tokens, full)
    total, keys_keep = lax.optimization_barrier((total, keys_keep))
    terms = [total[:, 0]] + [total[:, k].astype(jnp.bfloat16) for k in (1, 2, 3)]
    terms, full_1 = lax.optimization_barrier((terms, full))
    total = reduced(terms, 1)
    back = back_part(cotangent, full_1, 0, 8, ())
    total, back = lax.optimization_barrier((total, back))
    came = shift(total[1].astype(jnp.bfloat16), "l", 1)

    column = lax.dynamic_slice_in_dim(landing, me, 1, 1)[:, 0]
    lanes = jnp.arange(COUNT, dtype=jnp.int32)
    source = jnp.sum(jnp.where(column[None, :] == lanes[:, None], lanes[None, :], 0), axis=1, dtype=jnp.int32)
    new_weight, new_first, new_second = updated(me[None], source, moments, total[0], came, full, scale)
    keys = (keys_keep + keys_came).astype(jnp.bfloat16)
    return (keys, back, new_weight[None], new_first[None], new_second[None])


def solution(mesh):
    fine = Mesh(mesh.devices.reshape(SIZES), AXES)
    in_specs = (
        P(DP, "t"),
        P(DP, None),
        P("t", DP, None),
        P("t", DP, None),
        P("t", DP, None),
        P(),
    )
    out_specs = (
        P(DP, "t"),
        P(DP, "t"),
        P("t", DP, None),
        P("t", DP, None),
        P("t", DP, None),
    )
    return jax.shard_map(shards, mesh=fine, in_specs=in_specs, out_specs=out_specs, check_vma=False)
```

```python
import functools
import math

import jax
import jax.numpy as jnp
from jax import lax
from jax.experimental import pallas as pl
from jax.experimental.pallas import tpu as pltpu
from jax.sharding import Mesh, PartitionSpec as P

beta_first = 0.9
beta_second = 0.95
learn_rate = 0.001
decay_rate = 0.1
epsilon = 1e-08
bias_first = 1.0 - math.exp(100.0 * math.log(beta_first))
bias_second = 1.0 - math.exp(100.0 * math.log(beta_second))

AXES = ("z", "l", "x", "c", "t")
SIZES = (4, 2, 4, 2, 2)
DP = AXES[:4]
NZ, NL, NX, NC, NT = SIZES
COUNT = NZ * NL * NX * NC
NG = 2
SLOT = 64
TOP = 14.0
CODE = 16
MIB = 1 << 20


def shift(value, axis, step):
    size = SIZES[AXES.index(axis)]
    return lax.ppermute(value, axis, [(i, (i + step) % size) for i in range(size)])


def cross(value, stage, step):
    pairs = []
    for z in range(NZ):
        for x in range(NX):
            for c in range(NC):
                to = ((z + step) % NZ, x) if c == stage else (z, (x + step) % NX)
                pairs.append(((z * NX + x) * NC + c, (to[0] * NX + to[1]) * NC + c))
    return lax.ppermute(value, ("z", "x", "c"), pairs)


def gathered(value, stage):
    return [value] + [cross(value, stage, -k) for k in (1, 2, 3)]


def reduced(terms, stage):
    total = terms[0]
    for k in (1, 2, 3):
        total = total + cross(terms[k], stage, k).astype(jnp.float32)
    return total


def after(value, *others):
    return lax.optimization_barrier((value, *others))[0]


ANY = pl.BlockSpec(memory_space=pl.ANY)
SCALARS = pl.BlockSpec(memory_space=pltpu.SMEM)
AHEAD = 3


def kernel_call(kernel, out_shape, scratch, flops, moved, *args, out_specs=None, in_specs=None):
    return pl.pallas_call(
        kernel,
        in_specs=in_specs or [SCALARS] + [ANY] * (len(args) - 1),
        out_specs=out_specs or [ANY] * len(out_shape),
        out_shape=out_shape,
        scratch_shapes=scratch,
        compiler_params=pltpu.CompilerParams(vmem_limit_bytes=58 * MIB),
        cost_estimate=pl.CostEstimate(flops=flops, bytes_accessed=moved, transcendentals=0),
    )(*args)


def select_kernel(place, tokens, mine, other, held, low, high, in_sem, low_sem, high_sem):
    z, l, x, c = place[0], place[1], place[2], place[3]
    blocks, rows, _ = held.shape
    lanes = NC * SLOT
    below = lax.broadcasted_iota(jnp.int32, (rows, lanes), 1) < SLOT

    def load(k):
        return pltpu.make_async_copy(tokens.at[pl.ds(k * rows, rows)], held.at[k], in_sem.at[k])

    def store(k):
        return (
            pltpu.make_async_copy(low.at[k], mine.at[pl.ds(k * rows, rows)], low_sem.at[k]),
            pltpu.make_async_copy(high.at[k], other.at[pl.ds(k * rows, rows)], high_sem.at[k]),
        )

    def column(k, core, slot):
        first, pair, second = slot // (NL * 4), slot // 4 % NL, slot % 4
        to_z = lax.rem(z + jnp.where(core == 0, first, second), NZ)
        to_x = lax.rem(x + jnp.where(core == 0, second, first), NX)
        at = (to_z * NL + lax.rem(l + pair, NL)) * NX + to_x
        return held[k, :, pl.ds(pl.multiple_of(at * lanes, lanes), lanes)]

    for k in range(blocks):
        load(k).start()

    @pl.loop(0, blocks)
    def _(k):
        load(k).wait()
        for core, out in ((c, low), (1 - c, high)):
            for slot in range(0, COUNT // NC, NC):
                one = pltpu.roll(column(k, core, slot), SLOT * core, 1)
                two = pltpu.roll(column(k, core, slot + 1), SLOT * (1 - core), 1)
                out[k, :, slot * SLOT : (slot + 2) * SLOT] = jnp.where(below, one, two)
        for copy in store(k):
            copy.start()

    for k in range(blocks):
        for copy in store(k):
            copy.wait()


def selected(place, tokens):
    rows, half = tokens.shape
    blocks = 8
    out = jax.ShapeDtypeStruct((rows, half // NC), tokens.dtype)
    part = pltpu.VMEM((blocks, rows // blocks, half // NC), tokens.dtype)
    sems = pltpu.SemaphoreType.DMA((blocks,))
    scratch = [pltpu.VMEM((blocks, rows // blocks, half), tokens.dtype), part, part, sems, sems, sems]
    return kernel_call(select_kernel, [out, out], scratch, 0, 4 * rows * half, place, tokens)


def grad_kernel(mine, theirs, cot, cot_theirs, *refs):
    outs, refs = refs[:4], refs[4:]
    held, held_theirs, cots, own, sends, in_sem, theirs_sem, cot_sem, out_sem = refs
    blocks, _, block = held.shape

    def load(k):
        at = pl.ds(pl.multiple_of(k * block, block), block)
        return (
            pltpu.make_async_copy(mine.at[:, at], held.at[k], in_sem.at[k]),
            pltpu.make_async_copy(theirs.at[:, at], held_theirs.at[k], theirs_sem.at[k]),
        )

    def store(k):
        return pltpu.make_async_copy(own if k == 0 else sends.at[k - 1], outs[k], out_sem.at[k])

    both = [pltpu.make_async_copy(v, cots.at[n], cot_sem.at[n]) for n, v in enumerate((cot, cot_theirs))]
    first, second = load(0)
    both[0].start()
    first.start()
    both[1].start()
    second.start()
    for k in range(1, blocks):
        for copy in load(k):
            copy.start()

    over = (((0,), (0,)), ((), ()))

    @pl.loop(0, blocks)
    def _(k):
        one, two = load(k)
        pl.when(k == 0)(both[0].wait)
        one.wait()
        term = lax.dot_general(held[k], cots[0], over, preferred_element_type=jnp.float32)
        pl.when(k == 0)(both[1].wait)
        two.wait()
        term += lax.dot_general(held_theirs[k], cots[1], over, preferred_element_type=jnp.float32)
        term = term.reshape(own.shape)

        @pl.when(k == 0)
        def _():
            own[...] = term
            store(0).start()

        @pl.when(k > 0)
        def _():
            sends[k - 1] = term.astype(sends.dtype)

        for n in range(1, blocks):
            pl.when(k == n)(store(n).start)

    for k in range(blocks):
        store(k).wait()


def chip_grad(mine, theirs, cotangent, cotangent_theirs):
    rows, half = mine.shape
    width = cotangent.shape[1]
    piece = (half // 4 // SLOT, SLOT, width)
    part = pltpu.VMEM((4, rows, half // 4), mine.dtype)
    sems = pltpu.SemaphoreType.DMA((4,))
    scratch = [
        part,
        part,
        pltpu.VMEM((2, rows, width), mine.dtype),
        pltpu.VMEM(piece, jnp.float32),
        pltpu.VMEM((3, *piece), jnp.bfloat16),
        sems,
        sems,
        pltpu.SemaphoreType.DMA((2,)),
        sems,
    ]
    out_shape = [jax.ShapeDtypeStruct(piece, jnp.bfloat16 if n else jnp.float32) for n in range(4)]
    return kernel_call(
        grad_kernel,
        out_shape,
        scratch,
        0,
        0,
        mine,
        theirs,
        cotangent,
        cotangent_theirs,
        in_specs=[ANY] * 4,
    )


def reorder_kernel(place, target, tokens, *refs):
    pieces, refs = refs[: COUNT // 8], refs[COUNT // 8 :]
    full, keys_send, held, rows_in, moved, even, odd, acc, tokens_sem, rows_sem, full_sem = refs
    t = place[4]
    octets, _, block = held.shape
    lines = rows_in.shape[2]
    width = full.shape[1]
    column = width // NT

    def load(o):
        at = pl.multiple_of(o * lines, lines)
        copies = [
            pltpu.make_async_copy(p.at[pl.ds(at, lines)], rows_in.at[o, n], rows_sem.at[o, n])
            for n, p in enumerate(pieces)
        ]
        at = pl.multiple_of(o * block, block)
        return copies + [pltpu.make_async_copy(tokens.at[:, pl.ds(at, block)], held.at[o], tokens_sem.at[o])]

    def store(o):
        at = pl.ds(pl.multiple_of(o * block, block), block)
        return [
            pltpu.make_async_copy(
                moved.at[h, at], full.at[at, pl.ds(h * column, column)], full_sem.at[o, h]
            )
            for h in range(NT)
        ]

    for o in range(AHEAD):
        for copy in load(o):
            copy.start()
    acc[...] = jnp.zeros_like(acc)
    size, each = block // NG, lines // NG

    def arrive(o):
        @pl.when(o + AHEAD - 1 < octets)
        def _():
            for copy in load(o + AHEAD - 1):
                copy.start()

        for copy in load(o):
            copy.wait()

    def reorder(o, stage):
        for group in range(NG):
            rows = jnp.concatenate(
                [
                    rows_in[o, n, group * each : (group + 1) * each].reshape(-1, width)
                    for n in range(len(pieces))
                ],
                axis=0,
            )
            pick = lax.broadcasted_iota(jnp.int32, (size, rows.shape[0]), 0) == target[o * NG + group]
            pick = jnp.where(pick, 1.0, 0.0).astype(jnp.bfloat16)
            out = jnp.dot(pick, rows, preferred_element_type=jnp.float32).astype(jnp.bfloat16)
            at = pl.ds(pl.multiple_of(o * block + group * size, size), size)
            halves = [out[:, h * column : (h + 1) * column] for h in range(NT)]
            for h in range(NT):
                moved[h, at] = halves[h]
            stage[group * size : (group + 1) * size] = jnp.where(t == 0, halves[1], halves[0])

    def multiply(o, stage):
        acc[...] += jnp.dot(held[o], stage[...], preferred_element_type=jnp.float32)

    def leave(o):
        for copy in store(o):
            copy.start()

    for copy in load(0):
        copy.wait()
    reorder(0, even)
    leave(0)

    @pl.loop(0, octets // 2 - 1)
    def _(i):
        o = 2 * i
        arrive(o + 1)
        reorder(o + 1, odd)
        multiply(o, even)
        leave(o + 1)
        arrive(o + 2)
        reorder(o + 2, even)
        multiply(o + 1, odd)
        leave(o + 2)

    arrive(octets - 1)
    reorder(octets - 1, odd)
    multiply(octets - 2, even)
    leave(octets - 1)
    multiply(octets - 1, odd)
    power = jnp.floor(jnp.log2(jnp.clip(jnp.full((8, 128), jnp.max(jnp.abs(acc[...]))), 1e-30, None)))
    count = acc.shape[0]
    keys_send[:count] = acc[...] * jnp.exp2(TOP - power)[:1, :1]
    keys_send[count:] = jnp.broadcast_to(power[:1, :1], (keys_send.shape[0] - count, column))

    for o in range(octets):
        for copy in store(o):
            copy.wait()


def reorder_and_send(place, target, tokens, pieces):
    rows, half = tokens.shape
    width = pieces[0].shape[-1]
    octets = target.shape[0] // NG
    block = half // octets
    lines, line, _ = pieces[0].shape
    scratch = [
        pltpu.VMEM((octets, rows, block), tokens.dtype),
        pltpu.VMEM((octets, len(pieces), lines // octets, line, width), tokens.dtype),
        pltpu.VMEM((NT, half, width // NT), tokens.dtype),
        pltpu.VMEM((block, width // NT), tokens.dtype),
        pltpu.VMEM((block, width // NT), tokens.dtype),
        pltpu.VMEM((rows, width // NT), jnp.float32),
        pltpu.SemaphoreType.DMA((octets,)),
        pltpu.SemaphoreType.DMA((octets, len(pieces))),
        pltpu.SemaphoreType.DMA((octets, NT)),
    ]
    vmem = pl.BlockSpec(memory_space=pltpu.VMEM)
    return kernel_call(
        reorder_kernel,
        [
            jax.ShapeDtypeStruct((half, width), jnp.bfloat16),
            jax.ShapeDtypeStruct((rows + CODE, width // NT), jnp.float32),
        ],
        scratch,
        2 * rows * half * width,
        rows * half * 2 + half * width * 4,
        place,
        target,
        tokens,
        *pieces,
        in_specs=[SCALARS, vmem] + [ANY] * (1 + len(pieces)),
        out_specs=[ANY, vmem],
    )


def keep_kernel(place, tokens, full, keys, held, part, tokens_sem, part_sem):
    t = place[4]
    blocks, _, block = held.shape
    column = part.shape[2]

    def load(o):
        at = pl.ds(pl.multiple_of(o * block, block), block)
        return (
            pltpu.make_async_copy(
                full.at[at, pl.ds(pl.multiple_of(t * column, column), column)], part.at[o], part_sem.at[o]
            ),
            pltpu.make_async_copy(tokens.at[:, at], held.at[o], tokens_sem.at[o]),
        )

    for o in range(blocks):
        for copy in load(o):
            copy.start()
    keys[...] = jnp.zeros_like(keys)

    @pl.loop(0, blocks)
    def _(o):
        for copy in load(o):
            copy.wait()
        keys[...] += jnp.dot(held[o], part[o], preferred_element_type=jnp.float32)


def keys_kept(place, tokens, full):
    rows, half = tokens.shape
    width = full.shape[1]
    blocks = 4
    sems = pltpu.SemaphoreType.DMA((blocks,))
    return kernel_call(
        keep_kernel,
        jax.ShapeDtypeStruct((rows, width // NT), jnp.float32),
        [
            pltpu.VMEM((blocks, rows, half // blocks), tokens.dtype),
            pltpu.VMEM((blocks, half // blocks, width // NT), tokens.dtype),
            sems,
            sems,
        ],
        0,
        0,
        place,
        tokens,
        full,
        out_specs=pl.BlockSpec(memory_space=pltpu.VMEM),
    )


def back_kernel(first, cotangent, full, *refs):
    back, cot, held, out, cot_sem, in_sem, out_sem = refs[-7:]
    blocks, block, _ = held.shape

    def load(o):
        at = pl.ds(pl.multiple_of((first + o) * block, block), block)
        return pltpu.make_async_copy(full.at[at], held.at[o], in_sem.at[o])

    def store(o):
        at = pl.ds(pl.multiple_of((first + o) * block, block), block)
        return pltpu.make_async_copy(out.at[o], back.at[:, at], out_sem.at[o])

    whole = pltpu.make_async_copy(cotangent, cot, cot_sem)
    whole.start()
    for o in range(blocks):
        load(o).start()
    whole.wait()

    @pl.loop(0, blocks)
    def _(o):
        load(o).wait()
        out[o] = lax.dot_general(
            cot[...], held[o], (((1,), (1,)), ((), ())), preferred_element_type=jnp.float32
        ).astype(out.dtype)
        store(o).start()

    for o in range(blocks):
        store(o).wait()


def back_part(cotangent, full, first, last, held=()):
    rows, width = cotangent.shape
    half = full.shape[0]
    block = 512
    blocks = last - first
    sems = pltpu.SemaphoreType.DMA((blocks,))
    return pl.pallas_call(
        functools.partial(back_kernel, first),
        in_specs=[ANY] * (2 + len(held)),
        out_specs=ANY,
        out_shape=jax.ShapeDtypeStruct((rows, half), jnp.bfloat16),
        scratch_shapes=[
            pltpu.VMEM((rows, width), cotangent.dtype),
            pltpu.VMEM((blocks, block, width), full.dtype),
            pltpu.VMEM((blocks, rows, block), jnp.bfloat16),
            pltpu.SemaphoreType.DMA,
            sems,
            sems,
        ],
        input_output_aliases={2: 0} if held else {},
        compiler_params=pltpu.CompilerParams(vmem_limit_bytes=58 * MIB),
        cost_estimate=pl.CostEstimate(
            flops=2 * rows * block * blocks * width, bytes_accessed=0, transcendentals=0
        ),
    )(cotangent, full, *held)


def decoded(came):
    value = came.astype(jnp.float32)
    return value[:-CODE] * jnp.exp2(value[-CODE : 1 - CODE] - TOP)


def pack_kernel(first, second, out):
    for n, moment in enumerate((first, second)):
        for k in range(8):
            out[:, n * 8 + k, :] = moment[:, k * 128 : (k + 1) * 128]


def packed(first, second):
    rows, width = first.shape
    return pl.pallas_call(
        pack_kernel,
        out_shape=jax.ShapeDtypeStruct((rows, 16, width // 8), jnp.float32),
        compiler_params=pltpu.CompilerParams(vmem_limit_bytes=58 * MIB),
        cost_estimate=pl.CostEstimate(flops=0, bytes_accessed=4 * MIB // 4, transcendentals=0),
    )(first, second)


def update_kernel(scale, source, moments, own, came, full, weight, first, second, held):
    rows = held.shape[0]

    def move(p, carry):
        held[p] = moments[source[p]]
        return carry

    lax.fori_loop(0, rows, move, 0, unroll=8)
    for k in range(8):
        at = slice(k * 128, (k + 1) * 128)
        grad = (own[:, at] + came[:, at].astype(jnp.float32)) * scale
        base = full[:, at].astype(jnp.float32)
        new_first = beta_first * held[:, k, :] + (1.0 - beta_first) * grad
        new_second = beta_second * held[:, 8 + k, :] + (1.0 - beta_second) * grad * grad
        step = new_first / bias_first / (jnp.sqrt(new_second / bias_second) + epsilon)
        weight[:, at] = (base - learn_rate * (step + decay_rate * base)).astype(weight.dtype)
        first[:, at] = new_first
        second[:, at] = new_second


def updated(source, moments, own, came, base, scale):
    rows, width = own.shape
    whole = pl.BlockSpec((rows, width), lambda i, source: (0, 0))
    return pl.pallas_call(
        functools.partial(update_kernel, scale),
        grid_spec=pltpu.PrefetchScalarGridSpec(
            num_scalar_prefetch=1,
            grid=(1,),
            in_specs=[
                pl.BlockSpec(moments.shape, lambda i, source: (0, 0, 0)),
                whole,
                whole,
                whole,
            ],
            out_specs=[whole] * 3,
            scratch_shapes=[pltpu.VMEM(moments.shape, jnp.float32)],
        ),
        out_shape=[jax.ShapeDtypeStruct((rows, width), k) for k in (jnp.bfloat16, jnp.float32, jnp.float32)],
        compiler_params=pltpu.CompilerParams(vmem_limit_bytes=8 * MIB),
        cost_estimate=pl.CostEstimate(flops=0, bytes_accessed=MIB, transcendentals=0),
    )(source, moments, own, came, base)


def targets(landing, place, rows):
    z, l, x, c = place[0], place[1], place[2], place[3]
    steps = jnp.arange(4, dtype=jnp.int32)
    zs, xs = (z + steps) % NZ, (x + steps) % NX
    ls = (l + jnp.arange(NL, dtype=jnp.int32)) % NL

    def owners(core):
        along_z = (zs[None, :, None] * NL + ls) * NX + xs[:, None, None]
        along_x = (zs[:, None, None] * NL + ls) * NX + xs[None, :, None]
        return (jnp.where(core == 0, along_z, along_x) * NC + core).reshape(-1)

    order = jnp.concatenate([owners(c), owners(1 - c)])
    groups = 8 * NG
    each = COUNT // groups
    spots = jnp.take(landing, order, axis=0).reshape(COUNT // (4 * NL), 4 * NL, groups, each)
    spots = spots + jnp.arange(each, dtype=jnp.int32) * rows
    return spots.transpose(2, 0, 3, 1).reshape(groups, 1, each * COUNT)


def shards(tokens, cotangent, old_weight, old_first, old_second, landing):
    z, l, x, c, t = [lax.axis_index(a).astype(jnp.int32) for a in AXES]
    place = jnp.stack([z, l, x, c, t])
    me = ((z * NL + l) * NX + x) * NC + c
    rows, width = old_weight.shape[1:]
    scale = 1.0 / math.sqrt(tokens.shape[0] * COUNT)

    own = old_weight.reshape(rows, width)
    pair = jnp.stack([own, shift(own, "l", 1)])
    moments = packed(old_first.reshape(rows, width), old_second.reshape(rows, width))
    target = targets(landing, place, rows)
    pair, moments, target, place_1 = lax.optimization_barrier((pair, moments, target, place))
    line = jnp.stack(gathered(pair, 0)).reshape(4 * NL, rows, width)
    mine, other = selected(place_1, tokens)
    line, mine, other, cotangent_1, moments = lax.optimization_barrier((line, mine, other, cotangent, moments))
    theirs = shift(other, "c", 1)
    cotangent_theirs = shift(cotangent_1, "c", 1)
    line = line.transpose(1, 0, 2)
    here = gathered(line, 1)
    there = shift(line, "c", 1)
    moments = lax.all_to_all(moments, DP, split_axis=0, concat_axis=0, tiled=True)
    terms = chip_grad(mine, theirs, cotangent, cotangent_theirs)
    here, terms, moments = lax.optimization_barrier((here, terms, moments))
    pieces = here + [there] + [shift(v, "c", 1) for v in here[1:]]

    total = reduced(terms, 0).reshape(NL, 4, rows, width)
    full, keys_send = reorder_and_send(place, target, tokens, pieces)
    keys_came = shift(keys_send.astype(jnp.float16), "t", 1)
    keys_keep = keys_kept(place, tokens, full)
    total, keys_keep = lax.optimization_barrier((total, keys_keep))
    terms = [total[:, 0]] + [total[:, k].astype(jnp.bfloat16) for k in (1, 2, 3)]
    terms, full_1 = lax.optimization_barrier((terms, full))
    total = reduced(terms, 1)
    back = back_part(cotangent, full_1, 0, 4)
    total, back = lax.optimization_barrier((total, back))
    came = shift(total[1].astype(jnp.bfloat16), "l", 1)
    back = back_part(cotangent, full, 4, 8, (back,))

    base = lax.dynamic_slice_in_dim(full, me * rows, rows, 0)
    column = lax.dynamic_slice_in_dim(landing, me, 1, 1)[:, 0]
    lanes = jnp.arange(COUNT, dtype=jnp.int32)
    source = jnp.sum(jnp.where(column[None, :] == lanes[:, None], lanes[None, :], 0), axis=1, dtype=jnp.int32)
    new_weight, new_first, new_second = updated(source, moments, total[0], came, base, scale)
    keys = (keys_keep + decoded(keys_came)).astype(jnp.bfloat16)
    return (keys, back, new_weight[None], new_first[None], new_second[None])


def solution(mesh):
    fine = Mesh(mesh.devices.reshape(SIZES), AXES)
    in_specs = (
        P(DP, "t"),
        P(DP, None),
        P("t", DP, None),
        P("t", DP, None),
        P("t", DP, None),
        P(),
    )
    out_specs = (
        P(DP, "t"),
        P(DP, "t"),
        P("t", DP, None),
        P("t", DP, None),
        P("t", DP, None),
    )
    return jax.shard_map(shards, mesh=fine, in_specs=in_specs, out_specs=out_specs, check_vma=False)
```

```python
import functools
import math

import jax
import jax.numpy as jnp
import numpy as np
from jax import lax
from jax.experimental import pallas as pl
from jax.experimental.pallas import tpu as pltpu
from jax.sharding import Mesh, PartitionSpec as P

beta_first = 0.9
beta_second = 0.95
learn_rate = 0.001
decay_rate = 0.1
epsilon = 1e-08
bias_first = 1.0 - math.exp(100.0 * math.log(beta_first))
bias_second = 1.0 - math.exp(100.0 * math.log(beta_second))

AXES = ("z", "l", "x", "c", "t")
SIZES = (4, 2, 4, 2, 2)
DP = AXES[:4]
NZ, NL, NX, NC, NT = SIZES
COUNT = NZ * NL * NX * NC
NG = 2
SLOT = 64
TOP = 14.0
CODE = 16
MIB = 1 << 20


def shift(value, axis, step):
    size = SIZES[AXES.index(axis)]
    return lax.ppermute(value, axis, [(i, (i + step) % size) for i in range(size)])


def cross(value, stage, step):
    pairs = []
    for z in range(NZ):
        for x in range(NX):
            for c in range(NC):
                to = ((z + step) % NZ, x) if c == stage else (z, (x + step) % NX)
                pairs.append(((z * NX + x) * NC + c, (to[0] * NX + to[1]) * NC + c))
    return lax.ppermute(value, ("z", "x", "c"), pairs)


def gathered(value, stage):
    return [value] + [cross(value, stage, -k) for k in (1, 2, 3)]


def delivered(terms, stage):
    return [terms[0]] + [cross(terms[k], stage, k) for k in (1, 2, 3)]


def summed(terms):
    return sum(v.astype(jnp.float32) for v in terms[1:]) + terms[0]


ANY = pl.BlockSpec(memory_space=pl.ANY)
SCALARS = pl.BlockSpec(memory_space=pltpu.SMEM)
AHEAD = 2
PARTS = 1


def kernel_call(kernel, out_shape, scratch, flops, moved, *args, out_specs=None, in_specs=None, vmem=58):
    return pl.pallas_call(
        kernel,
        in_specs=in_specs or [SCALARS] + [ANY] * (len(args) - 1),
        out_specs=out_specs or [ANY] * len(out_shape),
        out_shape=out_shape,
        scratch_shapes=scratch,
        compiler_params=pltpu.CompilerParams(vmem_limit_bytes=vmem * MIB),
        cost_estimate=pl.CostEstimate(flops=flops, bytes_accessed=moved, transcendentals=0),
    )(*args)


def select_kernel(start, own, place, tokens, *refs):
    beside, (out, held, made, in_sem, beside_sem, out_sem) = refs[:-6], refs[-6:]
    z, x = place[0], place[2]
    core = place[3] if own else 1 - place[3]
    blocks, rows, half = held.shape
    lanes = NC * SLOT
    below = lax.broadcasted_iota(jnp.int32, (rows, lanes), 1) < SLOT

    def load(k):
        at = pl.ds(pl.multiple_of(start + k * rows, rows), rows)
        copies = [pltpu.make_async_copy(tokens.at[at], held.at[k], in_sem.at[k])]
        for v in beside:
            into = made.at[k, :, pl.ds(half // NC, v.shape[1])]
            copies.append(pltpu.make_async_copy(v.at[at], into, beside_sem.at[k]))
        return copies

    def store(k):
        return pltpu.make_async_copy(made.at[k], out.at[pl.ds(k * rows, rows)], out_sem.at[k])

    def column(k, slot):
        first, pair, second = slot // (NL * 4), slot // 4 % NL, slot % 4
        to_z = lax.rem(z + jnp.where(core == 0, first, second), NZ)
        to_x = lax.rem(x + jnp.where(core == 0, second, first), NX)
        at = (to_z * NL + lax.rem(place[1] + pair, NL)) * NX + to_x
        return held[k, :, pl.ds(pl.multiple_of(at * lanes, lanes), lanes)]

    for k in range(blocks):
        for copy in load(k):
            copy.start()

    @pl.loop(0, blocks)
    def _(k):
        for copy in load(k):
            copy.wait()
        for slot in range(0, COUNT // NC, NC):
            one = pltpu.roll(column(k, slot), SLOT * core, 1)
            two = pltpu.roll(column(k, slot + 1), SLOT * (1 - core), 1)
            made[k, :, slot * SLOT : (slot + 2) * SLOT] = jnp.where(below, one, two)
        store(k).start()

    for k in range(blocks):
        store(k).wait()


def selected(place, tokens, own, part, parts, *beside):
    rows, half = tokens.shape
    rows //= parts
    blocks = 8 // parts
    size = half // NC + sum(v.shape[1] for v in beside)
    scratch = [pltpu.VMEM((blocks, rows // blocks, n), tokens.dtype) for n in (half, size)]
    scratch += [pltpu.SemaphoreType.DMA((blocks,))] * 3
    kernel = functools.partial(select_kernel, part * rows, own)
    out = jax.ShapeDtypeStruct((rows, size), tokens.dtype)
    return kernel_call(kernel, out, scratch, 0, 2 * rows * half, place, tokens, *beside, out_specs=ANY)


def grad_kernel(mine, cot, *refs):
    theirs, refs = refs[:PARTS], refs[PARTS:]
    outs, refs = refs[:4], refs[4:]
    held, held_theirs, cots, own, sends, in_sem, theirs_sem, cot_sem, out_sem = refs
    blocks, _, block = held.shape
    rows = theirs[0].shape[0]
    parts = [pl.ds(p * rows, rows) for p in range(PARTS)]

    def load(k):
        at = pl.ds(pl.multiple_of(k * block, block), block)
        return [pltpu.make_async_copy(mine.at[:, at], held.at[k], in_sem.at[k])], [
            pltpu.make_async_copy(v.at[:, at], held_theirs.at[k, part], theirs_sem.at[k, p])
            for p, (v, part) in enumerate(zip(theirs, parts))
        ]

    def store(k):
        return pltpu.make_async_copy(own if k == 0 else sends.at[k - 1], outs[k], out_sem.at[k])

    beside = pl.ds(blocks * block, cot.shape[1])
    cot_copies = [pltpu.make_async_copy(cot, cots.at[0], cot_sem.at[0])], [
        pltpu.make_async_copy(v.at[:, beside], cots.at[1, part], cot_sem.at[1 + p])
        for p, (v, part) in enumerate(zip(theirs, parts))
    ]

    def start(copies):
        for copy in copies:
            copy.start()

    def wait(copies):
        for copy in copies:
            copy.wait()

    for n, copies in enumerate(load(0)):
        start(cot_copies[n])
        start(copies)
    over = (((0,), (0,)), ((), ()))

    @pl.loop(0, blocks)
    def _(k):
        @pl.when(k + 1 < blocks)
        def _():
            for copies in load(k + 1):
                start(copies)

        one, two = load(k)
        pl.when(k == 0)(lambda: wait(cot_copies[0]))
        wait(one)
        term = lax.dot_general(held[k], cots[0], over, preferred_element_type=jnp.float32)
        pl.when(k == 0)(lambda: wait(cot_copies[1]))
        wait(two)
        term += lax.dot_general(held_theirs[k], cots[1], over, preferred_element_type=jnp.float32)
        term = term.reshape(own.shape)

        @pl.when(k == 0)
        def _():
            own[...] = term
            store(0).start()

        @pl.when(k > 0)
        def _():
            sends[k - 1] = term.astype(sends.dtype)

        for n in range(1, blocks):
            pl.when(k == n)(store(n).start)

    for k in range(blocks):
        store(k).wait()


def chip_grad(mine, theirs, cotangent):
    rows, half = mine.shape
    width = cotangent.shape[1]
    piece = (half // 4 // SLOT, SLOT, width)
    part = pltpu.VMEM((4, rows, half // 4), mine.dtype)
    sems = pltpu.SemaphoreType.DMA((4,))
    scratch = [
        part,
        part,
        pltpu.VMEM((2, rows, width), mine.dtype),
        pltpu.VMEM(piece, jnp.float32),
        pltpu.VMEM((3, *piece), jnp.bfloat16),
        sems,
        pltpu.SemaphoreType.DMA((4, PARTS)),
        pltpu.SemaphoreType.DMA((1 + PARTS,)),
        sems,
    ]
    out_shape = [jax.ShapeDtypeStruct(piece, jnp.bfloat16 if n else jnp.float32) for n in range(4)]
    return kernel_call(
        grad_kernel,
        out_shape,
        scratch,
        0,
        0,
        mine,
        cotangent,
        *theirs,
        in_specs=[ANY] * (2 + PARTS),
    )


def reorder_kernel(place, target, tokens, *refs):
    pieces, refs = refs[: COUNT // 8], refs[COUNT // 8 :]
    full, keys_send, keys_keep, base, held, rows_in, moved, even, odd, acc, tokens_sem, rows_sem, full_sem, base_sem = refs
    t = place[4]
    octets, _, block = held.shape
    lines = rows_in.shape[2]
    width = full.shape[1]
    column = width // NT

    def load(o):
        at = pl.multiple_of(o * lines, lines)
        copies = [
            pltpu.make_async_copy(p.at[pl.ds(at, lines)], rows_in.at[o, n], rows_sem.at[o, n])
            for n, p in enumerate(pieces)
        ]
        at = pl.multiple_of(o * block, block)
        return copies + [pltpu.make_async_copy(tokens.at[:, pl.ds(at, block)], held.at[o], tokens_sem.at[o])]

    def store(o):
        at = pl.ds(pl.multiple_of(o * block, block), block)
        return [
            pltpu.make_async_copy(
                moved.at[h, at], full.at[at, pl.ds(h * column, column)], full_sem.at[o, h]
            )
            for h in range(NT)
        ]

    for o in range(AHEAD):
        for copy in load(o):
            copy.start()
    acc[...] = jnp.zeros_like(acc)
    keys_keep[...] = jnp.zeros_like(keys_keep)
    size, each = block // NG, lines // NG

    def arrive(o):
        @pl.when(o + AHEAD - 1 < octets)
        def _():
            for copy in load(o + AHEAD - 1):
                copy.start()

        for copy in load(o):
            copy.wait()

    def reorder(o, stage):
        for group in range(NG):
            rows = jnp.concatenate(
                [
                    rows_in[o, n, group * each : (group + 1) * each].reshape(-1, width)
                    for n in range(len(pieces))
                ],
                axis=0,
            )
            pick = lax.broadcasted_iota(jnp.int32, (size, rows.shape[0]), 0) == target[o * NG + group]
            pick = jnp.where(pick, 1.0, 0.0).astype(jnp.bfloat16)
            out = jnp.dot(pick, rows, preferred_element_type=jnp.float32).astype(jnp.bfloat16)
            at = pl.ds(pl.multiple_of(o * block + group * size, size), size)
            halves = [out[:, h * column : (h + 1) * column] for h in range(NT)]
            for h in range(NT):
                moved[h, at] = halves[h]
            at = slice(group * size, (group + 1) * size)
            stage[at, :column] = jnp.where(t == 0, halves[0], halves[1])
            stage[at, column:] = jnp.where(t == 0, halves[1], halves[0])

    def multiply(o, stage):
        term = jnp.dot(held[o], stage[...], preferred_element_type=jnp.float32)
        keys_keep[...] += term[:, :column]
        acc[...] += term[:, column:]

    def leave(o):
        for copy in store(o):
            copy.start()

    for copy in load(0):
        copy.wait()
    reorder(0, even)
    leave(0)

    @pl.loop(0, octets // 2 - 1)
    def _(i):
        o = 2 * i
        arrive(o + 1)
        reorder(o + 1, odd)
        multiply(o, even)
        leave(o + 1)
        arrive(o + 2)
        reorder(o + 2, even)
        multiply(o + 1, odd)
        leave(o + 2)

    arrive(octets - 1)
    reorder(octets - 1, odd)
    multiply(octets - 2, even)
    leave(octets - 1)
    me = ((place[0] * NL + place[1]) * NX + place[2]) * NC + place[3]
    own = [
        pltpu.make_async_copy(
            moved.at[h, pl.ds(pl.multiple_of(me * SLOT, SLOT), SLOT)],
            base.at[:, pl.ds(h * column, column)],
            base_sem.at[h],
        )
        for h in range(NT)
    ]
    for copy in own:
        copy.start()
    multiply(octets - 1, odd)
    power = jnp.floor(jnp.log2(jnp.clip(jnp.full((8, 128), jnp.max(jnp.abs(acc[...]))), 1e-30, None)))
    count = acc.shape[0]
    keys_send[:count] = acc[...] * jnp.exp2(TOP - power)[:1, :1]
    keys_send[count:] = jnp.broadcast_to(power[:1, :1], (keys_send.shape[0] - count, column))

    for copy in own:
        copy.wait()
    for o in range(octets):
        for copy in store(o):
            copy.wait()


def reorder_and_keys(place, target, tokens, pieces):
    rows, half = tokens.shape
    width = pieces[0].shape[-1]
    octets = target.shape[0] // NG
    block = half // octets
    lines, line, _ = pieces[0].shape
    scratch = [
        pltpu.VMEM((octets, rows, block), tokens.dtype),
        pltpu.VMEM((octets, len(pieces), lines // octets, line, width), tokens.dtype),
        pltpu.VMEM((NT, half, width // NT), tokens.dtype),
        pltpu.VMEM((block, width), tokens.dtype),
        pltpu.VMEM((block, width), tokens.dtype),
        pltpu.VMEM((rows, width // NT), jnp.float32),
        pltpu.SemaphoreType.DMA((octets,)),
        pltpu.SemaphoreType.DMA((octets, len(pieces))),
        pltpu.SemaphoreType.DMA((octets, NT)),
        pltpu.SemaphoreType.DMA((NT,)),
    ]
    vmem = pl.BlockSpec(memory_space=pltpu.VMEM)
    return kernel_call(
        reorder_kernel,
        [
            jax.ShapeDtypeStruct((half, width), jnp.bfloat16),
            jax.ShapeDtypeStruct((rows + CODE, width // NT), jnp.float32),
            jax.ShapeDtypeStruct((rows, width // NT), jnp.float32),
            jax.ShapeDtypeStruct((SLOT, width), jnp.bfloat16),
        ],
        scratch,
        3 * rows * half * width,
        rows * half * 2 + half * width * 4,
        place,
        target,
        tokens,
        *pieces,
        in_specs=[SCALARS, vmem] + [ANY] * (1 + len(pieces)),
        out_specs=[ANY, vmem, vmem, ANY],
        vmem=50,
    )


def back_kernel(first, cotangent, full, *refs):
    back, cot, held, out, cot_sem, in_sem, out_sem = refs[-7:]
    blocks, block, _ = held.shape

    def load(o):
        at = pl.ds(pl.multiple_of((first + o) * block, block), block)
        return pltpu.make_async_copy(full.at[at], held.at[o], in_sem.at[o])

    def store(o):
        at = pl.ds(pl.multiple_of((first + o) * block, block), block)
        return pltpu.make_async_copy(out.at[o], back.at[:, at], out_sem.at[o])

    whole = pltpu.make_async_copy(cotangent, cot, cot_sem)
    whole.start()
    load(0).start()
    whole.wait()

    @pl.loop(0, blocks)
    def _(o):
        @pl.when(o + 1 < blocks)
        def _():
            load(o + 1).start()

        load(o).wait()
        out[o] = lax.dot_general(
            cot[...], held[o], (((1,), (1,)), ((), ())), preferred_element_type=jnp.float32
        ).astype(out.dtype)
        store(o).start()

    for o in range(blocks):
        store(o).wait()


def back_part(cotangent, full, first, last, held=()):
    rows, width = cotangent.shape
    half = full.shape[0]
    block = 512
    blocks = last - first
    sems = pltpu.SemaphoreType.DMA((blocks,))
    return pl.pallas_call(
        functools.partial(back_kernel, first),
        in_specs=[ANY] * (2 + len(held)),
        out_specs=ANY,
        out_shape=jax.ShapeDtypeStruct((rows, half), jnp.bfloat16),
        scratch_shapes=[
            pltpu.VMEM((rows, width), cotangent.dtype),
            pltpu.VMEM((blocks, block, width), full.dtype),
            pltpu.VMEM((blocks, rows, block), jnp.bfloat16),
            pltpu.SemaphoreType.DMA,
            sems,
            sems,
        ],
        input_output_aliases={2: 0} if held else {},
        compiler_params=pltpu.CompilerParams(vmem_limit_bytes=58 * MIB),
        cost_estimate=pl.CostEstimate(
            flops=2 * rows * block * blocks * width, bytes_accessed=0, transcendentals=0
        ),
    )(cotangent, full, *held)


def decoded(came):
    power = came[-CODE : 1 - CODE].astype(jnp.float32)
    return came[:-CODE].astype(jnp.float32) * jnp.exp2(power - TOP)


def pack_kernel(first, second, out):
    for n, moment in enumerate((first, second)):
        for k in range(8):
            out[:, n * 8 + k, :] = moment[:, k * 128 : (k + 1) * 128]


def packed(first, second):
    rows, width = first.shape
    return pl.pallas_call(
        pack_kernel,
        out_shape=jax.ShapeDtypeStruct((rows, 16, width // 8), jnp.float32),
        compiler_params=pltpu.CompilerParams(vmem_limit_bytes=58 * MIB),
        cost_estimate=pl.CostEstimate(flops=0, bytes_accessed=4 * MIB // 4, transcendentals=0),
    )(first, second)


def update_kernel(scale, source, moments, own, came, full, weight, first, second, held):
    rows = held.shape[0]

    def move(p, carry):
        held[p] = moments[source[p]]
        return carry

    lax.fori_loop(0, rows, move, 0, unroll=8)
    for k in range(8):
        at = slice(k * 128, (k + 1) * 128)
        grad = (own[:, at] + came[:, at].astype(jnp.float32)) * scale
        base = full[:, at].astype(jnp.float32)
        new_first = beta_first * held[:, k, :] + (1.0 - beta_first) * grad
        new_second = beta_second * held[:, 8 + k, :] + (1.0 - beta_second) * grad * grad
        step = new_first / bias_first / (jnp.sqrt(new_second / bias_second) + epsilon)
        weight[:, at] = (base - learn_rate * (step + decay_rate * base)).astype(weight.dtype)
        first[:, at] = new_first
        second[:, at] = new_second


def updated(source, moments, own, came, base, scale):
    rows, width = own.shape
    whole = pl.BlockSpec((rows, width), lambda i, source: (0, 0))
    return pl.pallas_call(
        functools.partial(update_kernel, scale),
        grid_spec=pltpu.PrefetchScalarGridSpec(
            num_scalar_prefetch=1,
            grid=(1,),
            in_specs=[
                pl.BlockSpec(moments.shape, lambda i, source: (0, 0, 0)),
                whole,
                whole,
                whole,
            ],
            out_specs=[whole] * 3,
            scratch_shapes=[pltpu.VMEM(moments.shape, jnp.float32)],
        ),
        out_shape=[jax.ShapeDtypeStruct((rows, width), k) for k in (jnp.bfloat16, jnp.float32, jnp.float32)],
        compiler_params=pltpu.CompilerParams(vmem_limit_bytes=8 * MIB),
        cost_estimate=pl.CostEstimate(flops=0, bytes_accessed=MIB, transcendentals=0),
    )(source, moments, own, came, base)


def gather_orders():
    orders = []
    for me in range(COUNT):
        z, l, x, c = me // (NL * NX * NC), me // (NX * NC) % NL, me // NC % NX, me % NC
        order = []
        for core in (c, 1 - c):
            for second in range(4):
                for first in range(4):
                    dz, dx = (first, second) if core == 0 else (second, first)
                    for pair in range(NL):
                        to = (((z + dz) % NZ) * NL + (l + pair) % NL) * NX + (x + dx) % NX
                        order.append(to * NC + core)
        orders.append(order)
    return np.array(orders, np.int32)


def targets(landing, me, rows):
    order = lax.dynamic_slice_in_dim(jnp.asarray(gather_orders()), me, 1, 0)[0]
    groups = 8 * NG
    each = COUNT // groups
    spots = jnp.take(landing, order, axis=0).reshape(COUNT // (4 * NL), 4 * NL, groups, each)
    spots = spots + jnp.arange(each, dtype=jnp.int32) * rows
    return spots.transpose(2, 0, 3, 1).reshape(groups, 1, each * COUNT)


def shards(tokens, cotangent, old_weight, old_first, old_second, landing):
    z, l, x, c, t = [lax.axis_index(a).astype(jnp.int32) for a in AXES]
    place = jnp.stack([z, l, x, c, t])
    me = ((z * NL + l) * NX + x) * NC + c
    rows, width = old_weight.shape[1:]
    scale = 1.0 / math.sqrt(tokens.shape[0] * COUNT)

    own = old_weight.reshape(rows, width)
    pair = jnp.stack([own, shift(own, "l", 1)])
    moments = packed(old_first.reshape(rows, width), old_second.reshape(rows, width))
    target = targets(landing, me, rows)
    pair, moments, target, place_1 = lax.optimization_barrier((pair, moments, target, place))
    line = jnp.stack(gathered(pair, 0)).reshape(4 * NL, rows, width)
    other = selected(place_1, tokens, False, 0, PARTS, cotangent)
    line, other, place_2 = lax.optimization_barrier((line, other, place_1))
    theirs = shift(other, "c", 1)
    line = line.transpose(1, 0, 2)
    here = gathered(line, 1)
    there = shift(line, "c", 1)
    mine = selected(place_2, tokens, True, 0, 1)
    terms = chip_grad(mine, (theirs,), cotangent)
    here, there, terms, moments = lax.optimization_barrier((here, there, terms, moments))
    moments = lax.all_to_all(moments, DP, split_axis=0, concat_axis=0, tiled=True)
    pieces = here + [there] + [shift(v, "c", 1) for v in here[1:]]
    pieces, terms = lax.optimization_barrier((pieces, terms))

    terms = delivered(terms, 0)
    full, keys_send, keys_keep, base = reorder_and_keys(place, target, tokens, pieces)
    keys_came = shift(keys_send.astype(jnp.float16), "t", 1)
    terms, keys_keep, moments = lax.optimization_barrier((terms, keys_keep, moments))
    total = summed(terms).reshape(NL, 4, rows, width)
    terms = [total[:, 0]] + [total[:, k].astype(jnp.bfloat16) for k in (1, 2, 3)]
    terms, full_1 = lax.optimization_barrier((terms, full))
    terms = delivered(terms, 1)
    back = back_part(cotangent, full_1, 0, 4)
    terms, back = lax.optimization_barrier((terms, back))
    total = summed(terms)
    came = shift(total[1].astype(jnp.bfloat16), "l", 1)
    back = back_part(cotangent, full, 4, 8, (back,))
    came, keys_came, back = lax.optimization_barrier((came, keys_came, back))

    column = lax.dynamic_slice_in_dim(landing, me, 1, 1)[:, 0]
    lanes = jnp.arange(COUNT, dtype=jnp.int32)
    source = jnp.sum(jnp.where(column[None, :] == lanes[:, None], lanes[None, :], 0), axis=1, dtype=jnp.int32)
    new_weight, new_first, new_second = updated(source, moments, total[0], came, base, scale)
    keys = (keys_keep + decoded(keys_came)).astype(jnp.bfloat16)
    return (keys, back, new_weight[None], new_first[None], new_second[None])


def solution(mesh):
    fine = Mesh(mesh.devices.reshape(SIZES), AXES)
    in_specs = (
        P(DP, "t"),
        P(DP, None),
        P("t", DP, None),
        P("t", DP, None),
        P("t", DP, None),
        P(),
    )
    out_specs = (
        P(DP, "t"),
        P(DP, "t"),
        P("t", DP, None),
        P("t", DP, None),
        P("t", DP, None),
    )
    return jax.shard_map(shards, mesh=fine, in_specs=in_specs, out_specs=out_specs, check_vma=False)
```

```python
import functools
import math

import jax
import jax.numpy as jnp
import numpy as np
from jax import lax
from jax.experimental import pallas as pl
from jax.experimental.pallas import tpu as pltpu
from jax.sharding import Mesh, PartitionSpec as P

beta_first = 0.9
beta_second = 0.95
learn_rate = 0.001
decay_rate = 0.1
epsilon = 1e-08
bias_first = 1.0 - math.exp(100.0 * math.log(beta_first))
bias_second = 1.0 - math.exp(100.0 * math.log(beta_second))

AXES = ("z", "l", "x", "c", "t")
SIZES = (4, 2, 4, 2, 2)
DP = AXES[:4]
NZ, NL, NX, NC, NT = SIZES
COUNT = NZ * NL * NX * NC
NG = 2
SLOT = 64
TOP = 14.0
CODE = 16
MIB = 1 << 20


def shift(value, axis, step):
    size = SIZES[AXES.index(axis)]
    return lax.ppermute(value, axis, [(i, (i + step) % size) for i in range(size)])


def cross(value, stage, step):
    pairs = []
    for z in range(NZ):
        for x in range(NX):
            for c in range(NC):
                to = ((z + step) % NZ, x) if c == stage else (z, (x + step) % NX)
                pairs.append(((z * NX + x) * NC + c, (to[0] * NX + to[1]) * NC + c))
    return lax.ppermute(value, ("z", "x", "c"), pairs)


def gathered(value, stage):
    return [value] + [cross(value, stage, -k) for k in (1, 2, 3)]


def delivered(terms, stage):
    return [terms[0]] + [cross(terms[k], stage, k) for k in (1, 2, 3)]


def summed(terms):
    return sum(v.astype(jnp.float32) for v in terms[1:]) + terms[0]


ANY = pl.BlockSpec(memory_space=pl.ANY)
SCALARS = pl.BlockSpec(memory_space=pltpu.SMEM)
AHEAD = 3
PARTS = 1


def kernel_call(kernel, out_shape, scratch, flops, moved, *args, out_specs=None, in_specs=None, vmem=58):
    return pl.pallas_call(
        kernel,
        in_specs=in_specs or [SCALARS] + [ANY] * (len(args) - 1),
        out_specs=out_specs or [ANY] * len(out_shape),
        out_shape=out_shape,
        scratch_shapes=scratch,
        compiler_params=pltpu.CompilerParams(vmem_limit_bytes=vmem * MIB),
        cost_estimate=pl.CostEstimate(flops=flops, bytes_accessed=moved, transcendentals=0),
    )(*args)


def select_kernel(start, own, place, tokens, *refs):
    beside, (out, held, made, in_sem, beside_sem, out_sem) = refs[:-6], refs[-6:]
    z, x = place[0], place[2]
    core = place[3] if own else 1 - place[3]
    blocks, rows, half = held.shape
    lanes = NC * SLOT
    below = lax.broadcasted_iota(jnp.int32, (rows, lanes), 1) < SLOT

    def load(k):
        at = pl.ds(pl.multiple_of(start + k * rows, rows), rows)
        copies = [pltpu.make_async_copy(tokens.at[at], held.at[k], in_sem.at[k])]
        for v in beside:
            into = made.at[k, :, pl.ds(half // NC, v.shape[1])]
            copies.append(pltpu.make_async_copy(v.at[at], into, beside_sem.at[k]))
        return copies

    def store(k):
        return pltpu.make_async_copy(made.at[k], out.at[pl.ds(k * rows, rows)], out_sem.at[k])

    def column(k, slot):
        first, pair, second = slot // (NL * 4), slot // 4 % NL, slot % 4
        to_z = lax.rem(z + jnp.where(core == 0, first, second), NZ)
        to_x = lax.rem(x + jnp.where(core == 0, second, first), NX)
        at = (to_z * NL + lax.rem(place[1] + pair, NL)) * NX + to_x
        return held[k, :, pl.ds(pl.multiple_of(at * lanes, lanes), lanes)]

    for k in range(blocks):
        for copy in load(k):
            copy.start()

    @pl.loop(0, blocks)
    def _(k):
        for copy in load(k):
            copy.wait()
        for slot in range(0, COUNT // NC, NC):
            one = pltpu.roll(column(k, slot), SLOT * core, 1)
            two = pltpu.roll(column(k, slot + 1), SLOT * (1 - core), 1)
            made[k, :, slot * SLOT : (slot + 2) * SLOT] = jnp.where(below, one, two)
        store(k).start()

    for k in range(blocks):
        store(k).wait()


def selected(place, tokens, own, part, parts, *beside):
    rows, half = tokens.shape
    rows //= parts
    blocks = 8 // parts
    size = half // NC + sum(v.shape[1] for v in beside)
    scratch = [pltpu.VMEM((blocks, rows // blocks, n), tokens.dtype) for n in (half, size)]
    scratch += [pltpu.SemaphoreType.DMA((blocks,))] * 3
    kernel = functools.partial(select_kernel, part * rows, own)
    out = jax.ShapeDtypeStruct((rows, size), tokens.dtype)
    return kernel_call(kernel, out, scratch, 0, 2 * rows * half, place, tokens, *beside, out_specs=ANY)


def grad_kernel(mine, cot, *refs):
    theirs, refs = refs[:PARTS], refs[PARTS:]
    outs, refs = refs[:4], refs[4:]
    held, held_theirs, cots, own, sends, in_sem, theirs_sem, cot_sem, out_sem = refs
    blocks, _, block = held.shape
    rows = theirs[0].shape[0]
    parts = [pl.ds(p * rows, rows) for p in range(PARTS)]

    def load(k):
        at = pl.ds(pl.multiple_of(k * block, block), block)
        return [pltpu.make_async_copy(mine.at[:, at], held.at[k], in_sem.at[k])], [
            pltpu.make_async_copy(v.at[:, at], held_theirs.at[k, part], theirs_sem.at[k, p])
            for p, (v, part) in enumerate(zip(theirs, parts))
        ]

    def store(k):
        return pltpu.make_async_copy(own if k == 0 else sends.at[k - 1], outs[k], out_sem.at[k])

    beside = pl.ds(blocks * block, cot.shape[1])
    cot_copies = [pltpu.make_async_copy(cot, cots.at[0], cot_sem.at[0])], [
        pltpu.make_async_copy(v.at[:, beside], cots.at[1, part], cot_sem.at[1 + p])
        for p, (v, part) in enumerate(zip(theirs, parts))
    ]

    def start(copies):
        for copy in copies:
            copy.start()

    def wait(copies):
        for copy in copies:
            copy.wait()

    for n, copies in enumerate(load(0)):
        start(cot_copies[n])
        start(copies)
    over = (((0,), (0,)), ((), ()))

    @pl.loop(0, blocks)
    def _(k):
        @pl.when(k + 1 < blocks)
        def _():
            for copies in load(k + 1):
                start(copies)

        one, two = load(k)
        pl.when(k == 0)(lambda: wait(cot_copies[0]))
        wait(one)
        term = lax.dot_general(held[k], cots[0], over, preferred_element_type=jnp.float32)
        pl.when(k == 0)(lambda: wait(cot_copies[1]))
        wait(two)
        term += lax.dot_general(held_theirs[k], cots[1], over, preferred_element_type=jnp.float32)
        term = term.reshape(own.shape)

        @pl.when(k == 0)
        def _():
            own[...] = term
            store(0).start()

        @pl.when(k > 0)
        def _():
            sends[k - 1] = term.astype(sends.dtype)

        for n in range(1, blocks):
            pl.when(k == n)(store(n).start)

    for k in range(blocks):
        store(k).wait()


def chip_grad(mine, theirs, cotangent):
    rows, half = mine.shape
    width = cotangent.shape[1]
    piece = (half // 4 // SLOT, SLOT, width)
    part = pltpu.VMEM((4, rows, half // 4), mine.dtype)
    sems = pltpu.SemaphoreType.DMA((4,))
    scratch = [
        part,
        part,
        pltpu.VMEM((2, rows, width), mine.dtype),
        pltpu.VMEM(piece, jnp.float32),
        pltpu.VMEM((3, *piece), jnp.bfloat16),
        sems,
        pltpu.SemaphoreType.DMA((4, PARTS)),
        pltpu.SemaphoreType.DMA((1 + PARTS,)),
        sems,
    ]
    out_shape = [jax.ShapeDtypeStruct(piece, jnp.bfloat16 if n else jnp.float32) for n in range(4)]
    return kernel_call(
        grad_kernel,
        out_shape,
        scratch,
        0,
        0,
        mine,
        cotangent,
        *theirs,
        in_specs=[ANY] * (2 + PARTS),
    )


def reorder_kernel(place, target, tokens, *refs):
    pieces, refs = refs[: COUNT // 8], refs[COUNT // 8 :]
    full, keys_send, keys_keep, base, held, rows_in, moved, even, odd, acc, tokens_sem, rows_sem, full_sem, base_sem = refs
    t = place[4]
    octets, _, block = held.shape
    lines = rows_in.shape[2]
    width = full.shape[1]
    column = width // NT

    def load(o):
        at = pl.multiple_of(o * lines, lines)
        copies = [
            pltpu.make_async_copy(p.at[pl.ds(at, lines)], rows_in.at[o, n], rows_sem.at[o, n])
            for n, p in enumerate(pieces)
        ]
        at = pl.multiple_of(o * block, block)
        return copies + [pltpu.make_async_copy(tokens.at[:, pl.ds(at, block)], held.at[o], tokens_sem.at[o])]

    def store(o):
        at = pl.ds(pl.multiple_of(o * block, block), block)
        return [
            pltpu.make_async_copy(
                moved.at[h, at], full.at[at, pl.ds(h * column, column)], full_sem.at[o, h]
            )
            for h in range(NT)
        ]

    for o in range(AHEAD):
        for copy in load(o):
            copy.start()
    acc[...] = jnp.zeros_like(acc)
    keys_keep[...] = jnp.zeros_like(keys_keep)
    size, each = block // NG, lines // NG

    def arrive(o):
        @pl.when(o + AHEAD - 1 < octets)
        def _():
            for copy in load(o + AHEAD - 1):
                copy.start()

        for copy in load(o):
            copy.wait()

    def reorder(o, stage):
        for group in range(NG):
            rows = jnp.concatenate(
                [
                    rows_in[o, n, group * each : (group + 1) * each].reshape(-1, width)
                    for n in range(len(pieces))
                ],
                axis=0,
            )
            pick = lax.broadcasted_iota(jnp.int32, (size, rows.shape[0]), 0) == target[o * NG + group]
            pick = jnp.where(pick, 1.0, 0.0).astype(jnp.bfloat16)
            out = jnp.dot(pick, rows, preferred_element_type=jnp.float32).astype(jnp.bfloat16)
            at = pl.ds(pl.multiple_of(o * block + group * size, size), size)
            halves = [out[:, h * column : (h + 1) * column] for h in range(NT)]
            for h in range(NT):
                moved[h, at] = halves[h]
            at = slice(group * size, (group + 1) * size)
            stage[at, :column] = jnp.where(t == 0, halves[0], halves[1])
            stage[at, column:] = jnp.where(t == 0, halves[1], halves[0])

    def multiply(o, stage):
        term = jnp.dot(held[o], stage[...], preferred_element_type=jnp.float32)
        keys_keep[...] += term[:, :column]
        acc[...] += term[:, column:]

    def leave(o):
        for copy in store(o):
            copy.start()

    for copy in load(0):
        copy.wait()
    reorder(0, even)
    leave(0)

    @pl.loop(0, octets // 2 - 1)
    def _(i):
        o = 2 * i
        arrive(o + 1)
        reorder(o + 1, odd)
        multiply(o, even)
        leave(o + 1)
        arrive(o + 2)
        reorder(o + 2, even)
        multiply(o + 1, odd)
        leave(o + 2)

    arrive(octets - 1)
    reorder(octets - 1, odd)
    multiply(octets - 2, even)
    leave(octets - 1)
    me = ((place[0] * NL + place[1]) * NX + place[2]) * NC + place[3]
    own = [
        pltpu.make_async_copy(
            moved.at[h, pl.ds(pl.multiple_of(me * SLOT, SLOT), SLOT)],
            base.at[:, pl.ds(h * column, column)],
            base_sem.at[h],
        )
        for h in range(NT)
    ]
    for copy in own:
        copy.start()
    multiply(octets - 1, odd)
    power = jnp.floor(jnp.log2(jnp.clip(jnp.full((8, 128), jnp.max(jnp.abs(acc[...]))), 1e-30, None)))
    count = acc.shape[0]
    keys_send[:count] = acc[...] * jnp.exp2(TOP - power)[:1, :1]
    keys_send[count:] = jnp.broadcast_to(power[:1, :1], (keys_send.shape[0] - count, column))

    for copy in own:
        copy.wait()
    for o in range(octets):
        for copy in store(o):
            copy.wait()


def reorder_and_keys(place, target, tokens, pieces):
    rows, half = tokens.shape
    width = pieces[0].shape[-1]
    octets = target.shape[0] // NG
    block = half // octets
    lines, line, _ = pieces[0].shape
    scratch = [
        pltpu.VMEM((octets, rows, block), tokens.dtype),
        pltpu.VMEM((octets, len(pieces), lines // octets, line, width), tokens.dtype),
        pltpu.VMEM((NT, half, width // NT), tokens.dtype),
        pltpu.VMEM((block, width), tokens.dtype),
        pltpu.VMEM((block, width), tokens.dtype),
        pltpu.VMEM((rows, width // NT), jnp.float32),
        pltpu.SemaphoreType.DMA((octets,)),
        pltpu.SemaphoreType.DMA((octets, len(pieces))),
        pltpu.SemaphoreType.DMA((octets, NT)),
        pltpu.SemaphoreType.DMA((NT,)),
    ]
    vmem = pl.BlockSpec(memory_space=pltpu.VMEM)
    return kernel_call(
        reorder_kernel,
        [
            jax.ShapeDtypeStruct((half, width), jnp.bfloat16),
            jax.ShapeDtypeStruct((rows + CODE, width // NT), jnp.float32),
            jax.ShapeDtypeStruct((rows, width // NT), jnp.float32),
            jax.ShapeDtypeStruct((SLOT, width), jnp.bfloat16),
        ],
        scratch,
        3 * rows * half * width,
        rows * half * 2 + half * width * 4,
        place,
        target,
        tokens,
        *pieces,
        in_specs=[SCALARS, vmem] + [ANY] * (1 + len(pieces)),
        out_specs=[ANY, vmem, vmem, ANY],
        vmem=50,
    )


def back_kernel(first, cotangent, full, *refs):
    back, cot, held, out, cot_sem, in_sem, out_sem = refs[-7:]
    blocks, block, _ = held.shape

    def load(o):
        at = pl.ds(pl.multiple_of((first + o) * block, block), block)
        return pltpu.make_async_copy(full.at[at], held.at[o], in_sem.at[o])

    def store(o):
        at = pl.ds(pl.multiple_of((first + o) * block, block), block)
        return pltpu.make_async_copy(out.at[o], back.at[:, at], out_sem.at[o])

    whole = pltpu.make_async_copy(cotangent, cot, cot_sem)
    whole.start()
    load(0).start()
    whole.wait()

    @pl.loop(0, blocks)
    def _(o):
        @pl.when(o + 1 < blocks)
        def _():
            load(o + 1).start()

        load(o).wait()
        out[o] = lax.dot_general(
            cot[...], held[o], (((1,), (1,)), ((), ())), preferred_element_type=jnp.float32
        ).astype(out.dtype)
        store(o).start()

    for o in range(blocks):
        store(o).wait()


def back_part(cotangent, full, first, last, held=()):
    rows, width = cotangent.shape
    half = full.shape[0]
    block = 512
    blocks = last - first
    sems = pltpu.SemaphoreType.DMA((blocks,))
    return pl.pallas_call(
        functools.partial(back_kernel, first),
        in_specs=[ANY] * (2 + len(held)),
        out_specs=ANY,
        out_shape=jax.ShapeDtypeStruct((rows, half), jnp.bfloat16),
        scratch_shapes=[
            pltpu.VMEM((rows, width), cotangent.dtype),
            pltpu.VMEM((blocks, block, width), full.dtype),
            pltpu.VMEM((blocks, rows, block), jnp.bfloat16),
            pltpu.SemaphoreType.DMA,
            sems,
            sems,
        ],
        input_output_aliases={2: 0} if held else {},
        compiler_params=pltpu.CompilerParams(vmem_limit_bytes=40 * MIB),
        cost_estimate=pl.CostEstimate(
            flops=2 * rows * block * blocks * width, bytes_accessed=0, transcendentals=0
        ),
    )(cotangent, full, *held)


def decoded(came):
    power = came[-CODE : 1 - CODE].astype(jnp.float32)
    return came[:-CODE].astype(jnp.float32) * jnp.exp2(power - TOP)


def pack_kernel(first, second, out):
    for n, moment in enumerate((first, second)):
        for k in range(8):
            out[:, n * 8 + k, :] = moment[:, k * 128 : (k + 1) * 128]


def packed(first, second):
    rows, width = first.shape
    return pl.pallas_call(
        pack_kernel,
        out_shape=jax.ShapeDtypeStruct((rows, 16, width // 8), jnp.float32),
        compiler_params=pltpu.CompilerParams(vmem_limit_bytes=58 * MIB),
        cost_estimate=pl.CostEstimate(flops=0, bytes_accessed=4 * MIB // 4, transcendentals=0),
    )(first, second)


def update_kernel(scale, source, moments, own, came, full, weight, first, second, held):
    rows = held.shape[0]

    def move(p, carry):
        held[p] = moments[source[p]]
        return carry

    lax.fori_loop(0, rows, move, 0, unroll=8)
    for k in range(8):
        at = slice(k * 128, (k + 1) * 128)
        grad = (own[:, at] + came[:, at].astype(jnp.float32)) * scale
        base = full[:, at].astype(jnp.float32)
        new_first = beta_first * held[:, k, :] + (1.0 - beta_first) * grad
        new_second = beta_second * held[:, 8 + k, :] + (1.0 - beta_second) * grad * grad
        step = new_first / bias_first / (jnp.sqrt(new_second / bias_second) + epsilon)
        weight[:, at] = (base - learn_rate * (step + decay_rate * base)).astype(weight.dtype)
        first[:, at] = new_first
        second[:, at] = new_second


def updated(source, moments, own, came, base, scale):
    rows, width = own.shape
    whole = pl.BlockSpec((rows, width), lambda i, source: (0, 0))
    return pl.pallas_call(
        functools.partial(update_kernel, scale),
        grid_spec=pltpu.PrefetchScalarGridSpec(
            num_scalar_prefetch=1,
            grid=(1,),
            in_specs=[
                pl.BlockSpec(moments.shape, lambda i, source: (0, 0, 0)),
                whole,
                whole,
                whole,
            ],
            out_specs=[whole] * 3,
            scratch_shapes=[pltpu.VMEM(moments.shape, jnp.float32)],
        ),
        out_shape=[jax.ShapeDtypeStruct((rows, width), k) for k in (jnp.bfloat16, jnp.float32, jnp.float32)],
        compiler_params=pltpu.CompilerParams(vmem_limit_bytes=8 * MIB),
        cost_estimate=pl.CostEstimate(flops=0, bytes_accessed=MIB, transcendentals=0),
    )(source, moments, own, came, base)


def gather_orders():
    orders = []
    for me in range(COUNT):
        z, l, x, c = me // (NL * NX * NC), me // (NX * NC) % NL, me // NC % NX, me % NC
        order = []
        for core in (c, 1 - c):
            for second in range(4):
                for first in range(4):
                    dz, dx = (first, second) if core == 0 else (second, first)
                    for pair in range(NL):
                        to = (((z + dz) % NZ) * NL + (l + pair) % NL) * NX + (x + dx) % NX
                        order.append(to * NC + core)
        orders.append(order)
    return np.array(orders, np.int32)


def targets(landing, me, rows):
    order = lax.dynamic_slice_in_dim(jnp.asarray(gather_orders()), me, 1, 0)[0]
    groups = 8 * NG
    each = COUNT // groups
    spots = jnp.take(landing, order, axis=0).reshape(COUNT // (4 * NL), 4 * NL, groups, each)
    spots = spots + jnp.arange(each, dtype=jnp.int32) * rows
    return spots.transpose(2, 0, 3, 1).reshape(groups, 1, each * COUNT)


def shards(tokens, cotangent, old_weight, old_first, old_second, landing):
    z, l, x, c, t = [lax.axis_index(a).astype(jnp.int32) for a in AXES]
    place = jnp.stack([z, l, x, c, t])
    me = ((z * NL + l) * NX + x) * NC + c
    rows, width = old_weight.shape[1:]
    scale = 1.0 / math.sqrt(tokens.shape[0] * COUNT)

    own = old_weight.reshape(rows, width)
    pair = jnp.stack([own, shift(own, "l", 1)])
    moments = packed(old_first.reshape(rows, width), old_second.reshape(rows, width))
    target = targets(landing, me, rows)
    pair, moments, target, place_1 = lax.optimization_barrier((pair, moments, target, place))
    line = jnp.stack(gathered(pair, 0)).reshape(4 * NL, rows, width)
    other = selected(place_1, tokens, False, 0, PARTS, cotangent)
    line, other, place_2 = lax.optimization_barrier((line, other, place_1))
    theirs = shift(other, "c", 1)
    line = line.transpose(1, 0, 2)
    here = gathered(line, 1)
    there = shift(line, "c", 1)
    mine = selected(place_2, tokens, True, 0, 1)
    terms = chip_grad(mine, (theirs,), cotangent)
    here, there, terms, moments = lax.optimization_barrier((here, there, terms, moments))
    moments = lax.all_to_all(moments, DP, split_axis=0, concat_axis=0, tiled=True)
    pieces = here + [there] + [shift(v, "c", 1) for v in here[1:]]
    pieces, terms = lax.optimization_barrier((pieces, terms))

    terms = delivered(terms, 0)
    full, keys_send, keys_keep, base = reorder_and_keys(place, target, tokens, pieces)
    keys_came = shift(keys_send.astype(jnp.float16), "t", 1)
    terms, keys_keep, moments = lax.optimization_barrier((terms, keys_keep, moments))
    total = summed(terms).reshape(NL, 4, rows, width)
    terms = [total[:, 0]] + [total[:, k].astype(jnp.bfloat16) for k in (1, 2, 3)]
    terms, full_1 = lax.optimization_barrier((terms, full))
    terms = delivered(terms, 1)
    back = back_part(cotangent, full_1, 0, 4)
    terms, back = lax.optimization_barrier((terms, back))
    total = summed(terms)
    came = shift(total[1].astype(jnp.bfloat16), "l", 1)
    back = back_part(cotangent, full, 4, 8, (back,))
    came, keys_came, back = lax.optimization_barrier((came, keys_came, back))

    column = lax.dynamic_slice_in_dim(landing, me, 1, 1)[:, 0]
    lanes = jnp.arange(COUNT, dtype=jnp.int32)
    source = jnp.sum(jnp.where(column[None, :] == lanes[:, None], lanes[None, :], 0), axis=1, dtype=jnp.int32)
    new_weight, new_first, new_second = updated(source, moments, total[0], came, base, scale)
    keys = (keys_keep + decoded(keys_came)).astype(jnp.bfloat16)
    return (keys, back, new_weight[None], new_first[None], new_second[None])


def solution(mesh):
    fine = Mesh(mesh.devices.reshape(SIZES), AXES)
    in_specs = (
        P(DP, "t"),
        P(DP, None),
        P("t", DP, None),
        P("t", DP, None),
        P("t", DP, None),
        P(),
    )
    out_specs = (
        P(DP, "t"),
        P(DP, "t"),
        P("t", DP, None),
        P("t", DP, None),
        P("t", DP, None),
    )
    return jax.shard_map(shards, mesh=fine, in_specs=in_specs, out_specs=out_specs, check_vma=False)
```

```python
import functools
import math

import jax
import jax.numpy as jnp
import numpy as np
from jax import lax
from jax.experimental import pallas as pl
from jax.experimental.pallas import tpu as pltpu
from jax.sharding import Mesh, PartitionSpec as P

beta_first = 0.9
beta_second = 0.95
learn_rate = 0.001
decay_rate = 0.1
epsilon = 1e-08
bias_first = 1.0 - math.exp(100.0 * math.log(beta_first))
bias_second = 1.0 - math.exp(100.0 * math.log(beta_second))

AXES = ("z", "l", "x", "c", "t")
SIZES = (4, 2, 4, 2, 2)
DP = AXES[:4]
NZ, NL, NX, NC, NT = SIZES
COUNT = NZ * NL * NX * NC
NG = 2
SLOT = 64
TOP = 14.0
CODE = 16
MIB = 1 << 20


def shift(value, axis, step):
    size = SIZES[AXES.index(axis)]
    return lax.ppermute(value, axis, [(i, (i + step) % size) for i in range(size)])


def cross(value, stage, step):
    pairs = []
    for z in range(NZ):
        for x in range(NX):
            for c in range(NC):
                to = ((z + step) % NZ, x) if c == stage else (z, (x + step) % NX)
                pairs.append(((z * NX + x) * NC + c, (to[0] * NX + to[1]) * NC + c))
    return lax.ppermute(value, ("z", "x", "c"), pairs)


def gathered(value, stage):
    return [value] + [cross(value, stage, -k) for k in (1, 2, 3)]


def delivered(terms, stage):
    return [terms[0]] + [cross(terms[k], stage, k) for k in (1, 2, 3)]


def summed(terms):
    return sum(v.astype(jnp.float32) for v in terms[1:]) + terms[0]


ANY = pl.BlockSpec(memory_space=pl.ANY)
SCALARS = pl.BlockSpec(memory_space=pltpu.SMEM)
AHEAD = 4
PARTS = 1


def kernel_call(kernel, out_shape, scratch, flops, moved, *args, out_specs=None, in_specs=None, vmem=58):
    return pl.pallas_call(
        kernel,
        in_specs=in_specs or [SCALARS] + [ANY] * (len(args) - 1),
        out_specs=out_specs or [ANY] * len(out_shape),
        out_shape=out_shape,
        scratch_shapes=scratch,
        compiler_params=pltpu.CompilerParams(vmem_limit_bytes=vmem * MIB),
        cost_estimate=pl.CostEstimate(flops=flops, bytes_accessed=moved, transcendentals=0),
    )(*args)


def select_kernel(start, own, place, tokens, *refs):
    beside, (out, held, made, in_sem, beside_sem, out_sem) = refs[:-6], refs[-6:]
    z, x = place[0], place[2]
    core = place[3] if own else 1 - place[3]
    blocks, rows, half = held.shape
    lanes = NC * SLOT
    below = lax.broadcasted_iota(jnp.int32, (rows, lanes), 1) < SLOT

    def load(k):
        at = pl.ds(pl.multiple_of(start + k * rows, rows), rows)
        copies = [pltpu.make_async_copy(tokens.at[at], held.at[k], in_sem.at[k])]
        for v in beside:
            into = made.at[k, :, pl.ds(half // NC, v.shape[1])]
            copies.append(pltpu.make_async_copy(v.at[at], into, beside_sem.at[k]))
        return copies

    def store(k):
        return pltpu.make_async_copy(made.at[k], out.at[pl.ds(k * rows, rows)], out_sem.at[k])

    def column(k, slot):
        first, pair, second = slot // (NL * 4), slot // 4 % NL, slot % 4
        to_z = lax.rem(z + jnp.where(core == 0, first, second), NZ)
        to_x = lax.rem(x + jnp.where(core == 0, second, first), NX)
        at = (to_z * NL + lax.rem(place[1] + pair, NL)) * NX + to_x
        return held[k, :, pl.ds(pl.multiple_of(at * lanes, lanes), lanes)]

    for k in range(blocks):
        for copy in load(k):
            copy.start()

    @pl.loop(0, blocks)
    def _(k):
        for copy in load(k):
            copy.wait()
        for slot in range(0, COUNT // NC, NC):
            one = pltpu.roll(column(k, slot), SLOT * core, 1)
            two = pltpu.roll(column(k, slot + 1), SLOT * (1 - core), 1)
            made[k, :, slot * SLOT : (slot + 2) * SLOT] = jnp.where(below, one, two)
        store(k).start()

    for k in range(blocks):
        store(k).wait()


def selected(place, tokens, own, part, parts, *beside):
    rows, half = tokens.shape
    rows //= parts
    blocks = 8 // parts
    size = half // NC + sum(v.shape[1] for v in beside)
    scratch = [pltpu.VMEM((blocks, rows // blocks, n), tokens.dtype) for n in (half, size)]
    scratch += [pltpu.SemaphoreType.DMA((blocks,))] * 3
    kernel = functools.partial(select_kernel, part * rows, own)
    out = jax.ShapeDtypeStruct((rows, size), tokens.dtype)
    return kernel_call(kernel, out, scratch, 0, 2 * rows * half, place, tokens, *beside, out_specs=ANY)


def grad_kernel(mine, cot, *refs):
    theirs, refs = refs[:PARTS], refs[PARTS:]
    outs, refs = refs[:4], refs[4:]
    held, held_theirs, cots, own, sends, in_sem, theirs_sem, cot_sem, out_sem = refs
    blocks, _, block = held.shape
    rows = theirs[0].shape[0]
    parts = [pl.ds(p * rows, rows) for p in range(PARTS)]

    def load(k):
        at = pl.ds(pl.multiple_of(k * block, block), block)
        return [pltpu.make_async_copy(mine.at[:, at], held.at[k], in_sem.at[k])], [
            pltpu.make_async_copy(v.at[:, at], held_theirs.at[k, part], theirs_sem.at[k, p])
            for p, (v, part) in enumerate(zip(theirs, parts))
        ]

    def store(k):
        return pltpu.make_async_copy(own if k == 0 else sends.at[k - 1], outs[k], out_sem.at[k])

    beside = pl.ds(blocks * block, cot.shape[1])
    cot_copies = [pltpu.make_async_copy(cot, cots.at[0], cot_sem.at[0])], [
        pltpu.make_async_copy(v.at[:, beside], cots.at[1, part], cot_sem.at[1 + p])
        for p, (v, part) in enumerate(zip(theirs, parts))
    ]

    def start(copies):
        for copy in copies:
            copy.start()

    def wait(copies):
        for copy in copies:
            copy.wait()

    for n, copies in enumerate(load(0)):
        start(cot_copies[n])
        start(copies)
    over = (((0,), (0,)), ((), ()))

    @pl.loop(0, blocks)
    def _(k):
        @pl.when(k + 1 < blocks)
        def _():
            for copies in load(k + 1):
                start(copies)

        one, two = load(k)
        pl.when(k == 0)(lambda: wait(cot_copies[0]))
        wait(one)
        term = lax.dot_general(held[k], cots[0], over, preferred_element_type=jnp.float32)
        pl.when(k == 0)(lambda: wait(cot_copies[1]))
        wait(two)
        term += lax.dot_general(held_theirs[k], cots[1], over, preferred_element_type=jnp.float32)
        term = term.reshape(own.shape)

        @pl.when(k == 0)
        def _():
            own[...] = term
            store(0).start()

        @pl.when(k > 0)
        def _():
            sends[k - 1] = term.astype(sends.dtype)

        for n in range(1, blocks):
            pl.when(k == n)(store(n).start)

    for k in range(blocks):
        store(k).wait()


def chip_grad(mine, theirs, cotangent):
    rows, half = mine.shape
    width = cotangent.shape[1]
    piece = (half // 4 // SLOT, SLOT, width)
    part = pltpu.VMEM((4, rows, half // 4), mine.dtype)
    sems = pltpu.SemaphoreType.DMA((4,))
    scratch = [
        part,
        part,
        pltpu.VMEM((2, rows, width), mine.dtype),
        pltpu.VMEM(piece, jnp.float32),
        pltpu.VMEM((3, *piece), jnp.bfloat16),
        sems,
        pltpu.SemaphoreType.DMA((4, PARTS)),
        pltpu.SemaphoreType.DMA((1 + PARTS,)),
        sems,
    ]
    out_shape = [jax.ShapeDtypeStruct(piece, jnp.bfloat16 if n else jnp.float32) for n in range(4)]
    return kernel_call(
        grad_kernel,
        out_shape,
        scratch,
        0,
        0,
        mine,
        cotangent,
        *theirs,
        in_specs=[ANY] * (2 + PARTS),
    )


def reorder_kernel(place, target, tokens, *refs):
    pieces, refs = refs[: COUNT // 8], refs[COUNT // 8 :]
    full, keys_send, keys_keep, base, held, rows_in, moved, even, odd, acc, tokens_sem, rows_sem, full_sem, base_sem = refs
    t = place[4]
    octets, _, block = held.shape
    lines = rows_in.shape[2]
    width = full.shape[1]
    column = width // NT

    def load(o):
        at = pl.multiple_of(o * lines, lines)
        copies = [
            pltpu.make_async_copy(p.at[pl.ds(at, lines)], rows_in.at[o, n], rows_sem.at[o, n])
            for n, p in enumerate(pieces)
        ]
        at = pl.multiple_of(o * block, block)
        return copies + [pltpu.make_async_copy(tokens.at[:, pl.ds(at, block)], held.at[o], tokens_sem.at[o])]

    def store(o):
        at = pl.ds(pl.multiple_of(o * block, block), block)
        return [
            pltpu.make_async_copy(
                moved.at[h, at], full.at[at, pl.ds(h * column, column)], full_sem.at[o, h]
            )
            for h in range(NT)
        ]

    for o in range(AHEAD):
        for copy in load(o):
            copy.start()
    acc[...] = jnp.zeros_like(acc)
    keys_keep[...] = jnp.zeros_like(keys_keep)
    size, each = block // NG, lines // NG

    def arrive(o):
        @pl.when(o + AHEAD - 1 < octets)
        def _():
            for copy in load(o + AHEAD - 1):
                copy.start()

        for copy in load(o):
            copy.wait()

    def reorder(o, stage):
        for group in range(NG):
            rows = jnp.concatenate(
                [
                    rows_in[o, n, group * each : (group + 1) * each].reshape(-1, width)
                    for n in range(len(pieces))
                ],
                axis=0,
            )
            pick = lax.broadcasted_iota(jnp.int32, (size, rows.shape[0]), 0) == target[o * NG + group]
            pick = jnp.where(pick, 1.0, 0.0).astype(jnp.bfloat16)
            out = jnp.dot(pick, rows, preferred_element_type=jnp.float32).astype(jnp.bfloat16)
            at = pl.ds(pl.multiple_of(o * block + group * size, size), size)
            halves = [out[:, h * column : (h + 1) * column] for h in range(NT)]
            for h in range(NT):
                moved[h, at] = halves[h]
            at = slice(group * size, (group + 1) * size)
            stage[at, :column] = jnp.where(t == 0, halves[0], halves[1])
            stage[at, column:] = jnp.where(t == 0, halves[1], halves[0])

    def multiply(o, stage):
        term = jnp.dot(held[o], stage[...], preferred_element_type=jnp.float32)
        keys_keep[...] += term[:, :column]
        acc[...] += term[:, column:]

    def leave(o):
        for copy in store(o):
            copy.start()

    for copy in load(0):
        copy.wait()
    reorder(0, even)
    leave(0)

    @pl.loop(0, octets // 2 - 1)
    def _(i):
        o = 2 * i
        arrive(o + 1)
        reorder(o + 1, odd)
        multiply(o, even)
        leave(o + 1)
        arrive(o + 2)
        reorder(o + 2, even)
        multiply(o + 1, odd)
        leave(o + 2)

    arrive(octets - 1)
    reorder(octets - 1, odd)
    multiply(octets - 2, even)
    leave(octets - 1)
    me = ((place[0] * NL + place[1]) * NX + place[2]) * NC + place[3]
    own = [
        pltpu.make_async_copy(
            moved.at[h, pl.ds(pl.multiple_of(me * SLOT, SLOT), SLOT)],
            base.at[:, pl.ds(h * column, column)],
            base_sem.at[h],
        )
        for h in range(NT)
    ]
    for copy in own:
        copy.start()
    multiply(octets - 1, odd)
    power = jnp.floor(jnp.log2(jnp.clip(jnp.full((8, 128), jnp.max(jnp.abs(acc[...]))), 1e-30, None)))
    count = acc.shape[0]
    keys_send[:count] = acc[...] * jnp.exp2(TOP - power)[:1, :1]
    keys_send[count:] = jnp.broadcast_to(power[:1, :1], (keys_send.shape[0] - count, column))

    for copy in own:
        copy.wait()
    for o in range(octets):
        for copy in store(o):
            copy.wait()


def reorder_and_keys(place, target, tokens, pieces):
    rows, half = tokens.shape
    width = pieces[0].shape[-1]
    octets = target.shape[0] // NG
    block = half // octets
    lines, line, _ = pieces[0].shape
    scratch = [
        pltpu.VMEM((octets, rows, block), tokens.dtype),
        pltpu.VMEM((octets, len(pieces), lines // octets, line, width), tokens.dtype),
        pltpu.VMEM((NT, half, width // NT), tokens.dtype),
        pltpu.VMEM((block, width), tokens.dtype),
        pltpu.VMEM((block, width), tokens.dtype),
        pltpu.VMEM((rows, width // NT), jnp.float32),
        pltpu.SemaphoreType.DMA((octets,)),
        pltpu.SemaphoreType.DMA((octets, len(pieces))),
        pltpu.SemaphoreType.DMA((octets, NT)),
        pltpu.SemaphoreType.DMA((NT,)),
    ]
    vmem = pl.BlockSpec(memory_space=pltpu.VMEM)
    return kernel_call(
        reorder_kernel,
        [
            jax.ShapeDtypeStruct((half, width), jnp.bfloat16),
            jax.ShapeDtypeStruct((rows + CODE, width // NT), jnp.float32),
            jax.ShapeDtypeStruct((rows, width // NT), jnp.float32),
            jax.ShapeDtypeStruct((SLOT, width), jnp.bfloat16),
        ],
        scratch,
        3 * rows * half * width,
        rows * half * 2 + half * width * 4,
        place,
        target,
        tokens,
        *pieces,
        in_specs=[SCALARS, vmem] + [ANY] * (1 + len(pieces)),
        out_specs=[ANY, vmem, vmem, ANY],
        vmem=50,
    )


def back_kernel(first, cotangent, full, *refs):
    back, cot, held, out, cot_sem, in_sem, out_sem = refs[-7:]
    blocks, block, _ = held.shape

    def load(o):
        at = pl.ds(pl.multiple_of((first + o) * block, block), block)
        return pltpu.make_async_copy(full.at[at], held.at[o], in_sem.at[o])

    def store(o):
        at = pl.ds(pl.multiple_of((first + o) * block, block), block)
        return pltpu.make_async_copy(out.at[o], back.at[:, at], out_sem.at[o])

    whole = pltpu.make_async_copy(cotangent, cot, cot_sem)
    whole.start()
    load(0).start()
    whole.wait()

    @pl.loop(0, blocks)
    def _(o):
        @pl.when(o + 1 < blocks)
        def _():
            load(o + 1).start()

        load(o).wait()
        out[o] = lax.dot_general(
            cot[...], held[o], (((1,), (1,)), ((), ())), preferred_element_type=jnp.float32
        ).astype(out.dtype)
        store(o).start()

    for o in range(blocks):
        store(o).wait()


def back_part(cotangent, full, first, last, held=()):
    rows, width = cotangent.shape
    half = full.shape[0]
    block = 512
    blocks = last - first
    sems = pltpu.SemaphoreType.DMA((blocks,))
    return pl.pallas_call(
        functools.partial(back_kernel, first),
        in_specs=[ANY] * (2 + len(held)),
        out_specs=ANY,
        out_shape=jax.ShapeDtypeStruct((rows, half), jnp.bfloat16),
        scratch_shapes=[
            pltpu.VMEM((rows, width), cotangent.dtype),
            pltpu.VMEM((blocks, block, width), full.dtype),
            pltpu.VMEM((blocks, rows, block), jnp.bfloat16),
            pltpu.SemaphoreType.DMA,
            sems,
            sems,
        ],
        input_output_aliases={2: 0} if held else {},
        compiler_params=pltpu.CompilerParams(vmem_limit_bytes=28 * MIB),
        cost_estimate=pl.CostEstimate(
            flops=2 * rows * block * blocks * width, bytes_accessed=0, transcendentals=0
        ),
    )(cotangent, full, *held)


def decoded(came):
    power = came[-CODE : 1 - CODE].astype(jnp.float32)
    return came[:-CODE].astype(jnp.float32) * jnp.exp2(power - TOP)


def pack_kernel(first, second, out):
    for n, moment in enumerate((first, second)):
        for k in range(8):
            out[:, n * 8 + k, :] = moment[:, k * 128 : (k + 1) * 128]


def packed(first, second):
    rows, width = first.shape
    return pl.pallas_call(
        pack_kernel,
        out_shape=jax.ShapeDtypeStruct((rows, 16, width // 8), jnp.float32),
        compiler_params=pltpu.CompilerParams(vmem_limit_bytes=58 * MIB),
        cost_estimate=pl.CostEstimate(flops=0, bytes_accessed=4 * MIB // 4, transcendentals=0),
    )(first, second)


def update_kernel(scale, source, moments, own, came, full, weight, first, second, held):
    rows = held.shape[0]

    def move(p, carry):
        held[p] = moments[source[p]]
        return carry

    lax.fori_loop(0, rows, move, 0, unroll=8)
    for k in range(8):
        at = slice(k * 128, (k + 1) * 128)
        grad = (own[:, at] + came[:, at].astype(jnp.float32)) * scale
        base = full[:, at].astype(jnp.float32)
        new_first = beta_first * held[:, k, :] + (1.0 - beta_first) * grad
        new_second = beta_second * held[:, 8 + k, :] + (1.0 - beta_second) * grad * grad
        step = new_first / bias_first / (jnp.sqrt(new_second / bias_second) + epsilon)
        weight[:, at] = (base - learn_rate * (step + decay_rate * base)).astype(weight.dtype)
        first[:, at] = new_first
        second[:, at] = new_second


def updated(source, moments, own, came, base, scale):
    rows, width = own.shape
    whole = pl.BlockSpec((rows, width), lambda i, source: (0, 0))
    return pl.pallas_call(
        functools.partial(update_kernel, scale),
        grid_spec=pltpu.PrefetchScalarGridSpec(
            num_scalar_prefetch=1,
            grid=(1,),
            in_specs=[
                pl.BlockSpec(moments.shape, lambda i, source: (0, 0, 0)),
                whole,
                whole,
                whole,
            ],
            out_specs=[whole] * 3,
            scratch_shapes=[pltpu.VMEM(moments.shape, jnp.float32)],
        ),
        out_shape=[jax.ShapeDtypeStruct((rows, width), k) for k in (jnp.bfloat16, jnp.float32, jnp.float32)],
        compiler_params=pltpu.CompilerParams(vmem_limit_bytes=8 * MIB),
        cost_estimate=pl.CostEstimate(flops=0, bytes_accessed=MIB, transcendentals=0),
    )(source, moments, own, came, base)


def gather_orders():
    orders = []
    for me in range(COUNT):
        z, l, x, c = me // (NL * NX * NC), me // (NX * NC) % NL, me // NC % NX, me % NC
        order = []
        for core in (c, 1 - c):
            for second in range(4):
                for first in range(4):
                    dz, dx = (first, second) if core == 0 else (second, first)
                    for pair in range(NL):
                        to = (((z + dz) % NZ) * NL + (l + pair) % NL) * NX + (x + dx) % NX
                        order.append(to * NC + core)
        orders.append(order)
    return np.array(orders, np.int32)


def targets(landing, me, rows):
    order = lax.dynamic_slice_in_dim(jnp.asarray(gather_orders()), me, 1, 0)[0]
    groups = 8 * NG
    each = COUNT // groups
    spots = jnp.take(landing, order, axis=0).reshape(COUNT // (4 * NL), 4 * NL, groups, each)
    spots = spots + jnp.arange(each, dtype=jnp.int32) * rows
    return spots.transpose(2, 0, 3, 1).reshape(groups, 1, each * COUNT)


def shards(tokens, cotangent, old_weight, old_first, old_second, landing):
    z, l, x, c, t = [lax.axis_index(a).astype(jnp.int32) for a in AXES]
    place = jnp.stack([z, l, x, c, t])
    me = ((z * NL + l) * NX + x) * NC + c
    rows, width = old_weight.shape[1:]
    scale = 1.0 / math.sqrt(tokens.shape[0] * COUNT)

    own = old_weight.reshape(rows, width)
    pair = jnp.stack([own, shift(own, "l", 1)])
    moments = packed(old_first.reshape(rows, width), old_second.reshape(rows, width))
    target = targets(landing, me, rows)
    pair, moments, target, place_1 = lax.optimization_barrier((pair, moments, target, place))
    line = jnp.stack(gathered(pair, 0)).reshape(4 * NL, rows, width)
    other = selected(place_1, tokens, False, 0, PARTS, cotangent)
    line, other, place_2 = lax.optimization_barrier((line, other, place_1))
    theirs = shift(other, "c", 1)
    line = line.transpose(1, 0, 2)
    here = gathered(line, 1)
    there = shift(line, "c", 1)
    mine = selected(place_2, tokens, True, 0, 1)
    terms = chip_grad(mine, (theirs,), cotangent)
    here, there, terms, moments = lax.optimization_barrier((here, there, terms, moments))
    moments = lax.all_to_all(moments, DP, split_axis=0, concat_axis=0, tiled=True)
    pieces = here + [there] + [shift(v, "c", 1) for v in here[1:]]
    pieces, terms = lax.optimization_barrier((pieces, terms))

    terms = delivered(terms, 0)
    full, keys_send, keys_keep, base = reorder_and_keys(place, target, tokens, pieces)
    keys_came = shift(keys_send.astype(jnp.float16), "t", 1)
    terms, keys_keep, moments = lax.optimization_barrier((terms, keys_keep, moments))
    total = summed(terms).reshape(NL, 4, rows, width)
    terms = [total[:, 0]] + [total[:, k].astype(jnp.bfloat16) for k in (1, 2, 3)]
    terms, full_1 = lax.optimization_barrier((terms, full))
    terms = delivered(terms, 1)
    back = back_part(cotangent, full_1, 0, 4)
    terms, back = lax.optimization_barrier((terms, back))
    total = summed(terms)
    came = shift(total[1].astype(jnp.bfloat16), "l", 1)
    back = back_part(cotangent, full, 4, 8, (back,))
    came, keys_came, back = lax.optimization_barrier((came, keys_came, back))

    column = lax.dynamic_slice_in_dim(landing, me, 1, 1)[:, 0]
    lanes = jnp.arange(COUNT, dtype=jnp.int32)
    source = jnp.sum(jnp.where(column[None, :] == lanes[:, None], lanes[None, :], 0), axis=1, dtype=jnp.int32)
    new_weight, new_first, new_second = updated(source, moments, total[0], came, base, scale)
    keys = (keys_keep + decoded(keys_came)).astype(jnp.bfloat16)
    return (keys, back, new_weight[None], new_first[None], new_second[None])


def solution(mesh):
    fine = Mesh(mesh.devices.reshape(SIZES), AXES)
    in_specs = (
        P(DP, "t"),
        P(DP, None),
        P("t", DP, None),
        P("t", DP, None),
        P("t", DP, None),
        P(),
    )
    out_specs = (
        P(DP, "t"),
        P(DP, "t"),
        P("t", DP, None),
        P("t", DP, None),
        P("t", DP, None),
    )
    return jax.shard_map(shards, mesh=fine, in_specs=in_specs, out_specs=out_specs, check_vma=False)
```
